512 devices in a mesh: gx: 32 (over y, z_lo, core), gy: 16 (over z_hi, x).
Axes of the slice: x: 4, y: 8, z: 8 (z_hi: 4, z_lo: 2; z = z_hi * 2 + z_lo), core: 2. Of those that a mesh axis runs over, the one named last changes fastest.
Arguments:
- strain: float32 [5, 128, 256, 128], P(None, 'gx', 'gy'), may hold values from 0.0025 to 1
- coords: float32 [3, 128, 256, 128], P(None, 'gx', 'gy'), may hold values from -2 to 2560
- displacement: float32 [3, 128, 256, 128], P(None, 'gx', 'gy'), may hold values from -6 to 6
- stiffness: float32 [1, 128, 256, 128], P(None, 'gx', 'gy'), may hold values from 1 to 60
- neighbours: int32 [9, 128, 256], P(None, 'gx', 'gy'), may hold values from -1 to 32767, as said below
- corners: int32 [4, 128, 256, 128], P(None, 'gx', 'gy'), may hold values from 0 to 1151, as said below
Outputs:
- damage: float32 [5, 128, 256, 128], P(None, 'gx', 'gy')
- nodal_force: float32 [3, 128, 256, 128], P(None, 'gx', 'gy')
The draws below stay inside these ranges and needn't reach their ends.
Inputs may be any that keep to these rules, and one draw needn't show every extreme that they name: `neighbours`: slot 0 names the tile itself; slot k of 1 to 8 names the tile at the k-th of the row and column offsets (-1,-1), (-1,0), (-1,1), (0,-1), (0,1), (1,-1), (1,0), (1,1), or holds -1: always where that tile lies outside the grid, and for some links inside it. `corners`: entries are (3 * (dx + 1) + dy + 1) * 128 + s as in the reference program, with dx, dy in -1, 0, 1 and the named tile inside the grid.
All inputs are finite; a program needn't handle non-finite values.
Results may differ from the reference program's by a relative error of at most 0.0008.
Values may be sent and summed in bfloat16 or wider, within the bound.
No kernel may reach another device: no remote copies, remote signals or barrier semaphores. Data moves between devices by JAX's collectives and lax.ppermute only.
A program may use at most 64 MiB of HBM per device.

```python
import jax
import jax.numpy as jnp
from jax import lax

K = 9
PTS = 128
LAYERS = 5
NTX = 128
NTY = 256


TILE_MM = 10.0


OFFSET_ROWS = (-1, -1, -1, 0, 0, 1, 1, 1)


OFFSET_COLS = (-1, 0, 1, -1, 1, -1, 0, 1)


def draw_strain(key, part):
    key = jax.random.fold_in(key, 5)
    key_tile, key_shell = jax.random.split(key, 2)
    tile_level = jnp.exp(jax.random.uniform(key_tile, (1, NTX, NTY, 1), jnp.float32, minval=jnp.log(0.005), maxval=jnp.log(0.5)))
    shell_level = jnp.exp(jax.random.uniform(key_shell, (LAYERS, NTX, NTY, PTS), jnp.float32, minval=jnp.log(0.5), maxval=jnp.log(2.0)))
    return tile_level * shell_level


def draw_stiffness(key, part):
    key = jax.random.fold_in(key, 7)
    row_frac = jnp.arange(NTX, dtype=jnp.float32)[None, :, None, None] / max(NTX - 1, 1)
    col_frac = jnp.arange(NTY, dtype=jnp.float32)[None, None, :, None] / max(NTY - 1, 1)
    base = jax.random.uniform(key, (1, NTX, NTY, PTS), jnp.float32, minval=1.0, maxval=2.0)
    rising = (1.0 + 2.0 * row_frac) * (1.0 + 2.0 * col_frac)
    return base * rising


def draw_coords(key, part):
    key = jax.random.fold_in(key, 11)
    key_rows, key_cols, key_depth = jax.random.split(key, 3)
    grid_shape = (1, NTX, NTY, PTS)
    tile_rows = jnp.arange(NTX, dtype=jnp.float32)[None, :, None, None]
    tile_cols = jnp.arange(NTY, dtype=jnp.float32)[None, None, :, None]
    along_mm = (tile_rows + jax.random.uniform(key_rows, grid_shape, jnp.float32)) * TILE_MM
    across_mm = (tile_cols + jax.random.uniform(key_cols, grid_shape, jnp.float32)) * TILE_MM
    depth_mm = jax.random.uniform(key_depth, grid_shape, jnp.float32, minval=-2.0, maxval=2.0)
    return jnp.concatenate([along_mm, across_mm, depth_mm], axis=0)


def draw_neighbours(key, part):
    key = jax.random.fold_in(key, 23)
    step_rows = jnp.asarray(OFFSET_ROWS, jnp.int32)[:, None, None]
    step_cols = jnp.asarray(OFFSET_COLS, jnp.int32)[:, None, None]
    tile_rows = jnp.arange(NTX, dtype=jnp.int32)[None, :, None]
    tile_cols = jnp.arange(NTY, dtype=jnp.int32)[None, None, :]
    near_rows = tile_rows + step_rows
    near_cols = tile_cols + step_cols
    inside = (near_rows >= 0) & (near_rows < NTX) & (near_cols >= 0) & (near_cols < NTY)
    linked = jax.random.randint(key, (8, NTX, NTY), 0, 3) != 0
    others = jnp.where(inside & linked, near_rows * NTY + near_cols, -1)
    itself = jnp.broadcast_to(tile_rows * NTY + tile_cols, (1, NTX, NTY))
    return jnp.concatenate([itself, others], axis=0).astype(jnp.int32)


def draw_corners(key, part):
    key = jax.random.fold_in(key, 37)
    key_move, key_rows, key_cols, key_slot = jax.random.split(key, 4)
    grid_shape = (4, NTX, NTY, PTS)
    moving = (jax.random.randint(key_move, grid_shape, 0, 4) == 0).astype(jnp.int32)
    step_rows = jax.random.randint(key_rows, grid_shape, -1, 2) * moving
    step_cols = jax.random.randint(key_cols, grid_shape, -1, 2) * moving
    tile_rows = jnp.arange(NTX, dtype=jnp.int32)[None, :, None, None]
    tile_cols = jnp.arange(NTY, dtype=jnp.int32)[None, None, :, None]
    step_rows = jnp.where((tile_rows + step_rows < 0) | (tile_rows + step_rows >= NTX), 0, step_rows)
    step_cols = jnp.where((tile_cols + step_cols < 0) | (tile_cols + step_cols >= NTY), 0, step_cols)
    slot_of = jax.random.randint(key_slot, grid_shape, 0, PTS)
    codes = ((step_rows + 1) * 3 + step_cols + 1) * PTS + slot_of
    codes = codes.at[0, 0, 0, 0].set(9 * PTS - 1).at[1, 1, 1, 0].set(0)
    return codes.astype(jnp.int32)


def shard_levels(key, dims, pieces, low, top_value):
    def one(dim, blocks):
        heights = jax.random.uniform(jax.random.fold_in(jax.random.fold_in(key, 6), dim), (blocks,), jnp.float32, low / len(pieces), top_value / len(pieces))
        return jnp.repeat(jnp.exp(heights), dims[dim] // blocks).reshape((-1,) + (1,) * (len(dims) - dim - 1))

    gain = one(*pieces[0])
    for cut in pieces[1:]:
        gain = gain * one(*cut)
    return gain


def noise(own_key, shape, width, limit, shards=(), kind=jnp.bfloat16):
    loudness = shard_levels(own_key, shape, shards, -0.22, 0.18) if shards else 1.0
    entries = jax.random.normal(own_key, shape, jnp.float32) * width * loudness
    return jnp.minimum(jnp.maximum(entries, -limit), limit).astype(kind)


def setup_inputs(seed: int = 0) -> dict:
    key_of = jax.random.split(jax.random.key(seed), 7)
    strain = draw_strain(jax.random.fold_in(key_of[6], 71), 0)
    coords = draw_coords(jax.random.fold_in(key_of[6], 71), 0)
    displacement = noise(key_of[2], (3, NTX, NTY, PTS), 1.0, 6.0, ((1, 32), (2, 16)), jnp.float32)
    stiffness = draw_stiffness(jax.random.fold_in(key_of[6], 71), 0)
    neighbours = draw_neighbours(jax.random.fold_in(key_of[6], 71), 0)
    corners = draw_corners(jax.random.fold_in(key_of[6], 71), 0)
    return dict(strain=strain, coords=coords, displacement=displacement, stiffness=stiffness, neighbours=neighbours, corners=corners)


RADIUS_INV_SQ = 0.01
STRAIN_SCALE = 0.05
EDGE_PAIRS = ((0, 1), (1, 2), (2, 3), (3, 0))


def pair_weights(own_xyz, other_xyz, live_mask):
    dist_sq = (own_xyz[0][:, None, :] - other_xyz[0][:, :, None]) ** 2
    dist_sq = dist_sq + (own_xyz[1][:, None, :] - other_xyz[1][:, :, None]) ** 2
    dist_sq = dist_sq + (own_xyz[2][:, None, :] - other_xyz[2][:, :, None]) ** 2
    bell_curve = jnp.maximum(1.0 - dist_sq * RADIUS_INV_SQ, 0.0)
    return jnp.where(live_mask[:, None, None], bell_curve * bell_curve, 0.0).astype(jnp.bfloat16)


def reference(strain, coords, displacement, stiffness, neighbours, corners):
    ones_layer = jnp.ones((1, NTX, NTY, PTS), jnp.bfloat16)
    source = jnp.concatenate([strain.astype(jnp.bfloat16), ones_layer], axis=0).reshape(LAYERS + 1, NTX * NTY, PTS)
    flat_xyz = coords.reshape(3, NTX * NTY, PTS)

    def one_row(packed):
        row_lists, own_xyz = packed
        running = jnp.zeros((LAYERS + 1, NTY, PTS), jnp.float32)
        for slot_index in range(K):
            live_mask = row_lists[slot_index] >= 0
            safe_ids = jnp.where(live_mask, row_lists[slot_index], 0).astype(jnp.int32)
            values = jnp.take(source, safe_ids, axis=1)
            other_xyz = jnp.take(flat_xyz, safe_ids, axis=1)
            weights = pair_weights(own_xyz, other_xyz, live_mask)
            running = running + jnp.einsum("ctq,tqp->ctp", values.astype(jnp.float32), weights.astype(jnp.float32))
        return running

    totals = lax.map(one_row, (jnp.moveaxis(neighbours, 1, 0), jnp.moveaxis(coords, 1, 0)))
    averaged = totals[:, :LAYERS] / totals[:, LAYERS:]
    damage = jnp.moveaxis(averaged / (averaged + STRAIN_SCALE), 0, 1)

    strength = ((1.0 - jnp.mean(damage, axis=0)) * stiffness[0]).reshape(-1)
    top = jnp.max(strength)
    offset = corners // PTS
    slot_of = corners % PTS
    row_step = offset // 3 - 1
    col_step = offset % 3 - 1
    tile_rows = jnp.arange(NTX, dtype=jnp.int32)[None, :, None, None]
    tile_cols = jnp.arange(NTY, dtype=jnp.int32)[None, None, :, None]
    node_ids = (((tile_rows + row_step) * NTY + tile_cols + col_step) * PTS + slot_of).reshape(4, -1).astype(jnp.int32)
    flat_disp = displacement.reshape(3, -1)
    corner_disp = [jnp.take(flat_disp, node_ids[corner], axis=1) for corner in range(4)]
    forces = jnp.zeros((3, NTX * NTY * PTS), jnp.float32)
    for corner_from, corner_to in EDGE_PAIRS:
        spring = strength * (corner_disp[corner_to] - corner_disp[corner_from])
        forces = forces.at[:, node_ids[corner_from]].add(spring)
        forces = forces.at[:, node_ids[corner_to]].add(-spring)
    return damage, (forces / top).reshape(3, NTX, NTY, PTS)
```

```python
import jax
import jax.numpy as jnp
from jax import lax
from jax.experimental import pallas as pl
from jax.experimental.pallas import tpu as pltpu
from jax.sharding import PartitionSpec as P

PTS = 128
LAYERS = 5
ROWS = 4
COLS = 16
EXT_ROWS = ROWS + 2
EXT_COLS = COLS + 2
STRAIN_SCALE = 0.05
INV_RADIUS = 0.1
SPREAD_LIMIT = 128.0
SLOT_OF = {(0, 0): 0, (-1, -1): 1, (-1, 0): 2, (-1, 1): 3, (0, -1): 4, (0, 1): 5, (1, -1): 6, (1, 0): 7, (1, 1): 8}
PIECES = 32
SLAB = 8 * PIECES
RAW = 24
DISP_COLS = 24
FIELDS = 11
PAIRS = [(r + dr, r) for r in range(ROWS) for dr in range(3)]


def split3(value):
    hi = value.astype(jnp.bfloat16).astype(jnp.float32)
    rest = value - hi
    mid = rest.astype(jnp.bfloat16).astype(jnp.float32)
    return hi, mid, rest - mid


def body(
    strain, coords, disp, stiff, links, corners, before, after, left, right,
    damage, inner, rim_top, rim_bot, rim_left, rim_right, peak,
    sv, su, vt, block, weights, src, totals, strength, edisp, amounts, forces,
):
    f32, bf16 = jnp.float32, jnp.bfloat16
    gx, gy = lax.axis_index("gx"), lax.axis_index("gy")
    has_top, has_bot = gx > 0, gx < lax.axis_size("gx") - 1
    has_left, has_right = gy > 0, gy < lax.axis_size("gy") - 1

    row8 = lax.broadcasted_iota(jnp.int32, (8, PTS), 0)
    v_const = jnp.where((row8 >= 2) & (row8 <= 4), 1.0, 0.0).astype(f32)
    u_const = jnp.where(row8 >= 5, 1.0, 0.0).astype(f32)
    s_const = jnp.where(row8 == LAYERS, 1.0, 0.0).astype(f32)
    zero8 = jnp.zeros((8, PTS), f32)
    for c in range(EXT_COLS):
        for r in range(EXT_ROWS):
            sv[pl.ds(c * SLAB + r * PIECES + 16, 8), :] = v_const
            sv[pl.ds(c * SLAB + r * PIECES + 24, 8), :] = zero8
            src[pl.ds((c * EXT_ROWS + r) * 8, 8), :] = s_const
        for k in range(EXT_ROWS * PIECES, SLAB, 8):
            sv[pl.ds(c * SLAB + k, 8), :] = zero8
    for t in range(ROWS * COLS):
        su[pl.ds(t * PIECES + 16, 8), :] = u_const
        su[pl.ds(t * PIECES + 24, 8), :] = zero8
    block[...] = jnp.zeros(block.shape, bf16)
    forces[...] = jnp.zeros(forces.shape, f32)

    centre = [0.5 * (jnp.min(coords[x]) + jnp.max(coords[x])) for x in range(3)]

    def place(xyz, first, stride, count, own_first):
        a = [(xyz[x] - centre[x]) * INV_RADIUS for x in range(3)]
        norm = a[0] * a[0] + a[1] * a[1] + a[2] * a[2]
        for x in range(3):
            hi, mid, lo = split3(a[x])
            for k, v in zip((0, 3, 6, 9, 12, 15), (hi, hi, mid, mid, hi, lo)):
                sv[pl.ds(first + k + x, count, stride=stride), :] = v
            sv[pl.ds(first + RAW + x, count, stride=stride), :] = xyz[x]
            if own_first is not None:
                for k, v in zip((0, 3, 6, 9, 12, 15), (hi, mid, hi, mid, lo, hi)):
                    su[pl.ds(own_first + k + x, count, stride=ROWS * PIECES), :] = 2.0 * v
        for k, v in enumerate(split3(-norm)):
            sv[pl.ds(first + 21 + k, count, stride=stride), :] = v
        if own_first is not None:
            for k, v in enumerate(split3(1.0 - norm)):
                su[pl.ds(own_first + 18 + k, count, stride=ROWS * PIECES), :] = v
        return norm

    far = jnp.zeros((8, PTS), f32)
    for r in range(ROWS):
        norm = place([coords[x, r] for x in range(3)], SLAB + (r + 1) * PIECES, SLAB, COLS, r * PIECES)
        far = jnp.maximum(far, jnp.maximum(norm[0:8], norm[8:16]))
    for halo, r, there in ((before, 0, has_top), (after, EXT_ROWS - 1, has_bot)):
        norm = place([halo[x] for x in range(3)], SLAB + r * PIECES, SLAB, COLS, None)
        norm = jnp.where(there, norm, 0.0)
        far = jnp.maximum(far, jnp.maximum(norm[0:8], norm[8:16]))
    rows6 = lax.broadcasted_iota(jnp.int32, (EXT_ROWS, PTS), 0)
    inside6 = ((rows6 > 0) | has_top) & ((rows6 < EXT_ROWS - 1) | has_bot)
    side = jnp.zeros((EXT_ROWS, PTS), f32)
    for halo, c, there in ((left, 0, has_left), (right, EXT_COLS - 1, has_right)):
        norm = place([halo[x] for x in range(3)], c * SLAB, PIECES, EXT_ROWS, None)
        side = jnp.maximum(side, jnp.where(inside6 & there, norm, 0.0))
    spread = jnp.maximum(jnp.max(far), jnp.max(side))
    near = spread <= SPREAD_LIMIT

    for l in range(LAYERS):
        for r in range(EXT_ROWS):
            row = before[3 + l] if r == 0 else after[3 + l] if r == EXT_ROWS - 1 else strain[l, r - 1]
            src[pl.ds((EXT_ROWS + r) * 8 + l, COLS, stride=EXT_ROWS * 8), :] = row
        src[pl.ds(l, EXT_ROWS, stride=8), :] = left[3 + l]
        src[pl.ds((EXT_COLS - 1) * EXT_ROWS * 8 + l, EXT_ROWS, stride=8), :] = right[3 + l]
    for x in range(3):
        for r in range(EXT_ROWS):
            row = before[8 + x] if r == 0 else after[8 + x] if r == EXT_ROWS - 1 else disp[x, r - 1]
            edisp[pl.ds((x * EXT_ROWS + r) * DISP_COLS + 1, COLS), :] = row
        edisp[pl.ds(x * EXT_ROWS * DISP_COLS, EXT_ROWS, stride=DISP_COLS), :] = left[8 + x]
        edisp[pl.ds(x * EXT_ROWS * DISP_COLS + COLS + 1, EXT_ROWS, stride=DISP_COLS), :] = right[8 + x]

    def live(dr, dc, r, c):
        return jnp.where(links[SLOT_OF[(dr, dc)], r, c] >= 0, 1.0, 0.0).astype(f32)

    @pl.when(near)
    def _():
        def turn(c, carry):
            slab = sv[pl.ds(pl.multiple_of(c * SLAB, SLAB), SLAB), :]
            vt[pl.ds(pl.multiple_of(c * PTS, PTS), PTS), :] = slab.T.astype(bf16)
            return carry

        lax.fori_loop(0, EXT_COLS, turn, 0, unroll=6)

        def column(c, carry):
            for j, (ext, r) in enumerate(PAIRS):
                own = su[pl.ds(pl.multiple_of((c * ROWS + r) * PIECES, PIECES), PIECES), :]
                block[pl.ds(ext * PIECES, PIECES), pl.ds(j * PTS, PTS)] = own.astype(bf16)
            sums = [zero8 for _ in range(ROWS)]
            near_cols = vt[pl.ds(pl.multiple_of(c * PTS, PTS), 3 * PTS), :]
            for j in range(0, len(PAIRS), 2):
                bell = jnp.dot(near_cols, block[:, j * PTS : (j + 2) * PTS], preferred_element_type=f32)
                bell = jnp.maximum(bell, 0.0)
                weights[:, j * PTS : (j + 2) * PTS] = (bell * bell).astype(bf16)
            for j in range(0, len(PAIRS), 2):
                halves = []
                for ext, r in PAIRS[j : j + 2]:
                    parts = []
                    for dc in range(3):
                        at = pl.multiple_of(((c + dc) * EXT_ROWS + ext) * 8, 8)
                        parts.append(src[pl.ds(at, 8), :] * live(ext - r - 1, dc - 1, r, c))
                    halves.append(jnp.concatenate(parts, axis=1))
                values = jnp.concatenate(halves, axis=0).astype(bf16)
                out = jnp.dot(values, weights[:, j * PTS : (j + 2) * PTS], preferred_element_type=f32)
                for h in range(2):
                    r = PAIRS[j + h][1]
                    sums[r] = sums[r] + out[8 * h : 8 * h + 8, h * PTS : (h + 1) * PTS]
            for r in range(ROWS):
                totals[pl.ds(r * COLS + c, 8, stride=ROWS * COLS), :] = sums[r]
            return carry

        lax.fori_loop(0, COLS, column, 0, unroll=2)

    @pl.when(jnp.logical_not(near))
    def _():
        def tile(t, carry):
            r, c = t // COLS, t % COLS
            own = sv[pl.ds(pl.multiple_of((c + 1) * SLAB + (r + 1) * PIECES + RAW, 8), 8), :]
            total = zero8
            for (dr, dc), slot in SLOT_OF.items():
                at = pl.multiple_of((c + 1 + dc) * SLAB + (r + 1 + dr) * PIECES + RAW, 8)
                other = sv[pl.ds(at, 8), :]
                turned = jnp.concatenate([other] + [zero8] * 15, axis=0).T
                dist = jnp.zeros((PTS, PTS), f32)
                for x in range(3):
                    dist = dist + (own[x : x + 1, :] - turned[:, x : x + 1]) ** 2
                bell = jnp.maximum(1.0 - dist * 0.01, 0.0)
                pair = (bell * bell).astype(bf16)
                at = pl.multiple_of(((c + 1 + dc) * EXT_ROWS + r + 1 + dr) * 8, 8)
                values = src[pl.ds(at, 8), :] * jnp.where(links[slot, r, c] >= 0, 1.0, 0.0)
                total = total + jnp.dot(values.astype(bf16), pair, preferred_element_type=f32)
            totals[pl.ds(t, 8, stride=ROWS * COLS), :] = total
            return carry

        lax.fori_loop(0, ROWS * COLS, tile, 0)

    top = jnp.zeros((COLS, PTS), f32)
    for r in range(ROWS):
        weight_sum = totals[pl.ds(LAYERS * ROWS * COLS + r * COLS, COLS), :]
        mean = jnp.zeros((COLS, PTS), f32)
        for l in range(LAYERS):
            averaged = totals[pl.ds(l * ROWS * COLS + r * COLS, COLS), :] / weight_sum
            value = averaged / (averaged + STRAIN_SCALE)
            damage[l, r] = value
            mean = mean + value
        power = (1.0 - mean / LAYERS) * stiff[0, r]
        strength[r] = power
        top = jnp.maximum(top, power) if r else power
    peak[...] = jnp.full(peak.shape, jnp.max(top), f32)

    def gather(r, carry):
        for g in range(COLS // 8):
            power = strength[r, 8 * g : 8 * g + 8, :]
            codes = [corners[k, r, 8 * g : 8 * g + 8, :] for k in range(4)]
            offset = [code >> 7 for code in codes]
            slot = [code & (PTS - 1) for code in codes]
            at = [
                pl.ds(pl.multiple_of(((r * COLS + 8 * g) * 4 + k) * 8, 8) + i, 8, stride=32)
                for k in range(4) for i in range(8)
            ]
            for k in range(4):
                amounts[at[8 * k + 3], :] = offset[k].astype(f32)
                amounts[at[8 * k + 7], :] = slot[k].astype(f32)
            for x in range(3):
                picked = []
                base = (x * EXT_ROWS + r) * DISP_COLS + 8 * g
                table = [edisp[pl.ds(base + (o // 3) * DISP_COLS + o % 3, 8), :] for o in range(9)]
                for k in range(4):
                    found = jnp.take_along_axis(table[0], slot[k], axis=1)
                    for o in range(1, 9):
                        found = jnp.where(offset[k] == o, jnp.take_along_axis(table[o], slot[k], axis=1), found)
                    picked.append(found)
                springs = [power * (picked[(k + 1) % 4] - picked[k]) for k in range(4)]
                for k in range(4):
                    amount = springs[k] - springs[(k + 3) % 4]
                    hi = amount.astype(bf16).astype(f32)
                    amounts[at[8 * k + x], :] = hi
                    amounts[at[8 * k + 4 + x], :] = amount - hi
        return carry

    lax.fori_loop(0, ROWS, gather, 0, unroll=2)

    nodes = lax.broadcasted_iota(jnp.int32, (PTS, PTS), 0).astype(f32)

    def scatter(t, carry):
        r, c = t // COLS, t % COLS
        picks, rows = [], []
        for k in range(4):
            own = amounts[pl.ds(pl.multiple_of((t * 4 + k) * 8, 8), 8), :]
            offset, slot = own[3:4, :], own[7:8, :]
            rows.append(jnp.concatenate([jnp.where(offset == float(o), own, 0.0) for o in range(10)], axis=0))
            picks.append(jnp.where(slot == nodes, 1.0, 0.0).astype(bf16))
        left_side = jnp.concatenate(rows, axis=1).astype(bf16)
        right_side = jnp.concatenate(picks, axis=1)
        out = lax.dot_general(left_side, right_side, (((1,), (1,)), ((), ())), preferred_element_type=f32)
        for o in range(9):
            at = pl.ds(pl.multiple_of(((r + o // 3) * EXT_COLS + c + o % 3) * 8, 8), 8)
            forces[at, :] = forces[at, :] + out[8 * o : 8 * o + 8]
        return carry

    lax.fori_loop(0, ROWS * COLS, scatter, 0, unroll=8)

    def node_sum(x, first, count, stride):
        return (
            forces[pl.ds(first * 8 + x, count, stride=8 * stride), :]
            + forces[pl.ds(first * 8 + 4 + x, count, stride=8 * stride), :]
        )

    for x in range(3):
        for r in range(ROWS):
            inner[x, r] = node_sum(x, (r + 1) * EXT_COLS + 1, COLS, 1)
        rim_top[x] = node_sum(x, 0, EXT_COLS, 1).astype(bf16)
        rim_bot[x] = node_sum(x, (EXT_ROWS - 1) * EXT_COLS, EXT_COLS, 1).astype(bf16)
        rim_left[x] = node_sum(x, EXT_COLS, ROWS, EXT_COLS)
        rim_right[x] = node_sum(x, 2 * EXT_COLS - 1, ROWS, EXT_COLS)


def block_step(strain, coords, disp, stiff, links, corners, before, after, left, right, peers):
    f32 = jnp.float32
    vmem = pl.BlockSpec(memory_space=pltpu.VMEM)
    specs = [vmem] * 10
    specs[4] = pl.BlockSpec(memory_space=pltpu.SMEM)
    outs = (
        jax.ShapeDtypeStruct((LAYERS, ROWS, COLS, PTS), f32),
        jax.ShapeDtypeStruct((3, ROWS, COLS, PTS), f32),
        jax.ShapeDtypeStruct((3, EXT_COLS, PTS), jnp.bfloat16),
        jax.ShapeDtypeStruct((3, EXT_COLS, PTS), jnp.bfloat16),
        jax.ShapeDtypeStruct((3, ROWS, PTS), f32),
        jax.ShapeDtypeStruct((3, ROWS, PTS), f32),
        jax.ShapeDtypeStruct((peers, PTS), f32),
    )
    scratch = [
        pltpu.VMEM((EXT_COLS * SLAB, PTS), f32),
        pltpu.VMEM((COLS * ROWS * PIECES, PTS), f32),
        pltpu.VMEM((EXT_COLS * PTS, SLAB), jnp.bfloat16),
        pltpu.VMEM((SLAB, len(PAIRS) * PTS), jnp.bfloat16),
        pltpu.VMEM((3 * PTS, len(PAIRS) * PTS), jnp.bfloat16),
        pltpu.VMEM((EXT_COLS * EXT_ROWS * 8, PTS), f32),
        pltpu.VMEM((8 * ROWS * COLS, PTS), f32),
        pltpu.VMEM((ROWS, COLS, PTS), f32),
        pltpu.VMEM((3 * EXT_ROWS * DISP_COLS, PTS), f32),
        pltpu.VMEM((ROWS * COLS * 32, PTS), f32),
        pltpu.VMEM((EXT_ROWS * EXT_COLS * 8, PTS), f32),
    ]
    return pl.pallas_call(
        body,
        out_shape=outs,
        in_specs=specs,
        out_specs=(vmem,) * 7,
        scratch_shapes=scratch,
        compiler_params=pltpu.CompilerParams(vmem_limit_bytes=40 * 1024 * 1024),
        name="block_step",
    )(strain, coords, disp, stiff, links, corners, before, after, left, right)


def exchange(last, first, axis):
    peers = lax.axis_size(axis)
    up = [(i, i + 1) for i in range(peers - 1)]
    return lax.ppermute(last, axis, up), lax.ppermute(first, axis, [(j, i) for i, j in up])


def local(strain, coords, displacement, stiffness, neighbours, corners):
    peers_x, peers_y = lax.axis_size("gx"), lax.axis_size("gy")
    own = (coords, strain, displacement)

    def row(r):
        return jnp.concatenate([v[:, r] for v in own], axis=0)

    def column(c):
        mid = jnp.concatenate([v[:, :, c] for v in own], axis=0)
        return jnp.concatenate([before[:, None, c], mid, after[:, None, c]], axis=1)

    before, after = exchange(row(ROWS - 1), row(0), "gx")
    left, right = exchange(column(COLS - 1), column(0), "gy")
    damage, inner, rim_top, rim_bot, rim_left, rim_right, peak = block_step(
        strain, coords, displacement, stiffness, neighbours, corners, before, after, left, right, peers_x
    )
    from_above, from_below = exchange(rim_bot, rim_top, "gx")
    peaks = lax.all_to_all(peak, "gx", 0, 0, tiled=True)
    from_above, from_below = from_above.astype(jnp.float32), from_below.astype(jnp.float32)

    def side(rim, c):
        return rim.at[:, 0].add(from_above[:, c]).at[:, ROWS - 1].add(from_below[:, c])

    from_left, from_right = exchange(side(rim_right, EXT_COLS - 1), side(rim_left, 0), "gy")
    peak = jnp.broadcast_to(jnp.max(peaks, axis=0, keepdims=True), (peers_y, PTS))
    top = jnp.max(lax.all_to_all(peak, "gy", 0, 0, tiled=True))
    inner = inner.at[:, 0].add(from_above[:, 1:-1]).at[:, ROWS - 1].add(from_below[:, 1:-1])
    inner = inner.at[:, :, 0].add(from_left).at[:, :, COLS - 1].add(from_right)
    return damage, inner / top


def solution(mesh):
    spec = P(None, "gx", "gy", None)
    in_specs = (spec, spec, spec, spec, P(None, "gx", "gy"), spec)
    return jax.shard_map(local, mesh=mesh, in_specs=in_specs, out_specs=(spec, spec), check_vma=False)
```

```python
import jax
import jax.numpy as jnp
from jax import lax
from jax.experimental import pallas as pl
from jax.experimental.pallas import tpu as pltpu
from jax.sharding import PartitionSpec as P

PTS = 128
LAYERS = 5
ROWS = 4
COLS = 16
EXT_ROWS = ROWS + 2
LAST = ROWS + 1
EXT_COLS = COLS + 2
STRAIN_SCALE = 0.05
INV_RADIUS = 0.1
SPREAD_LIMIT = 128.0
SLOT_OF = {(0, 0): 0, (-1, -1): 1, (-1, 0): 2, (-1, 1): 3, (0, -1): 4, (0, 1): 5, (1, -1): 6, (1, 0): 7, (1, 1): 8}
PIECES = 32
RAW = 24
TILES = ROWS * COLS
DISP_COLS = 24
INSIDE = [(o, r) for r in range(ROWS) for o in range(ROWS) if abs(o - r) <= 1]
V_ROWS = (0, 3, 6, 9, 12, 15)
MIB = 1024 * 1024


def split3(value):
    hi = value.astype(jnp.bfloat16).astype(jnp.float32)
    rest = value - hi
    mid = rest.astype(jnp.bfloat16).astype(jnp.float32)
    return hi, mid, rest - mid


def scaled(xyz, centre):
    a = [(xyz[x] - centre[x]) * INV_RADIUS for x in range(3)]
    return a, a[0] * a[0] + a[1] * a[1] + a[2] * a[2]


def centre_of(coords):
    return [0.5 * (jnp.min(coords[x]) + jnp.max(coords[x])) for x in range(3)]


def put_other(sv, a, norm, at):
    for x in range(3):
        hi, mid, lo = split3(a[x])
        for k, v in zip(V_ROWS, (hi, hi, mid, mid, hi, lo)):
            sv[at(k + x), :] = v
    for k, v in enumerate(split3(-norm)):
        sv[at(21 + k), :] = v


def put_own(su, a, norm, xyz, at):
    for x in range(3):
        hi, mid, lo = split3(a[x])
        for k, v in zip(V_ROWS, (hi, mid, hi, mid, lo, hi)):
            su[at(k + x), :] = 2.0 * v
        su[at(RAW + x), :] = xyz[x]
    for k, v in enumerate(split3(1.0 - norm)):
        su[at(18 + k), :] = v


def constant_rows():
    row8 = lax.broadcasted_iota(jnp.int32, (8, PTS), 0)
    other = jnp.where((row8 >= 2) & (row8 <= 4), 1.0, 0.0)
    own = jnp.where(row8 >= 5, 1.0, 0.0)
    ones = jnp.where(row8 == LAYERS, 1.0, 0.0)
    return other.astype(jnp.float32), own.astype(jnp.float32), ones.astype(jnp.float32)


def rows_at(index, size, count=None):
    return pl.ds(pl.multiple_of(index * size, size), size if count is None else count)


def bell_weights(other, own):
    bell = jnp.maximum(jnp.dot(other, own, preferred_element_type=jnp.float32), 0.0)
    return (bell * bell).astype(jnp.bfloat16)


def direct_total(own, other, values):
    turned = jnp.concatenate([other] + [jnp.zeros((8, PTS), jnp.float32)] * 15, axis=0).T
    dist = jnp.zeros((PTS, PTS), jnp.float32)
    for x in range(3):
        dist = dist + (own[x : x + 1, :] - turned[:, x : x + 1]) ** 2
    bell = jnp.maximum(1.0 - dist * 0.01, 0.0)
    pair = (bell * bell).astype(jnp.bfloat16)
    return jnp.dot(values.astype(jnp.bfloat16), pair, preferred_element_type=jnp.float32)


def is_live(links, dr, dc, r, c):
    return jnp.where(links[SLOT_OF[(dr, dc)], r, c] >= 0, 1.0, 0.0).astype(jnp.float32)


def facing(first, second, axis):
    even = lax.axis_index(axis) % 2 == 0
    return (lambda i: jnp.where(even, second[i], first[i])), (lambda i: jnp.where(even, first[i], second[i]))


def inside_body(strain, coords, links, totals, sv, su, vt, block, weights, src):
    f32, bf16 = jnp.float32, jnp.bfloat16
    other_const, own_const, ones = constant_rows()
    zero8 = jnp.zeros((8, PTS), f32)
    for c in range(EXT_COLS):
        edge = c in (0, EXT_COLS - 1)
        for r in range(ROWS):
            src[pl.ds((c * ROWS + r) * 8, 8), :] = zero8 if edge else ones
            if not edge:
                sv[pl.ds(((c - 1) * ROWS + r) * PIECES + 16, 8), :] = other_const
                sv[pl.ds(((c - 1) * ROWS + r) * PIECES + 24, 8), :] = zero8
    for t in range(TILES):
        su[pl.ds(t * PIECES + 16, 8), :] = own_const
        su[pl.ds(t * PIECES + 24, 8), :] = zero8
    for c in (0, EXT_COLS - 1):
        vt[pl.ds(c * PTS, PTS), :] = jnp.zeros((PTS, PTS), bf16)
    block[...] = jnp.zeros(block.shape, bf16)

    centre = centre_of(coords)
    far = jnp.zeros((COLS, PTS), f32)
    step = ROWS * PIECES
    for r in range(ROWS):
        xyz = [coords[x, r] for x in range(3)]
        a, norm = scaled(xyz, centre)
        far = jnp.maximum(far, norm)
        put_other(sv, a, norm, lambda k: pl.ds(r * PIECES + k, COLS, stride=step))
        put_own(su, a, norm, xyz, lambda k: pl.ds(r * PIECES + k, COLS, stride=step))
        for l in range(LAYERS):
            src[pl.ds((ROWS + r) * 8 + l, COLS, stride=ROWS * 8), :] = strain[l, r]
    near = jnp.max(far) <= SPREAD_LIMIT

    @pl.when(near)
    def _():
        def turn(c, carry):
            vt[rows_at(c + 1, PTS), :] = sv[rows_at(c, step), :].T.astype(bf16)
            return carry

        lax.fori_loop(0, COLS, turn, 0, unroll=8)

        def column(c, carry):
            for j, (o, r) in enumerate(INSIDE):
                own = su[rows_at(c * ROWS + r, PIECES), :]
                block[pl.ds(o * PIECES, PIECES), pl.ds(j * PTS, PTS)] = own.astype(bf16)
            others = vt[rows_at(c, PTS, 3 * PTS), :]
            for j in range(0, len(INSIDE), 2):
                weights[:, j * PTS : (j + 2) * PTS] = bell_weights(others, block[:, j * PTS : (j + 2) * PTS])
            sums = [zero8 for _ in range(ROWS)]
            for j in range(0, len(INSIDE), 2):
                halves = []
                for o, r in INSIDE[j : j + 2]:
                    parts = [src[rows_at((c + dc) * ROWS + o, 8), :] * is_live(links, o - r, dc - 1, r, c) for dc in range(3)]
                    halves.append(jnp.concatenate(parts, axis=1))
                values = jnp.concatenate(halves, axis=0).astype(bf16)
                out = jnp.dot(values, weights[:, j * PTS : (j + 2) * PTS], preferred_element_type=f32)
                for h in range(2):
                    r = INSIDE[j + h][1]
                    sums[r] = sums[r] + out[8 * h : 8 * h + 8, h * PTS : (h + 1) * PTS]
            for r in range(ROWS):
                totals[pl.ds(r * COLS + c, 8, stride=TILES), :] = sums[r]
            return carry

        lax.fori_loop(0, COLS, column, 0, unroll=2)

    @pl.when(jnp.logical_not(near))
    def _():
        def tile(t, carry):
            r, c = t // COLS, t % COLS
            own = su[pl.ds(pl.multiple_of((c * ROWS + r) * PIECES + RAW, 8), 8), :]
            total = zero8
            for (dr, dc), slot in SLOT_OF.items():
                within = (r + dr >= 0) & (r + dr < ROWS) & (c + dc >= 0) & (c + dc < COLS) & (links[slot, r, c] >= 0)
                o = jnp.minimum(jnp.maximum(r + dr, 0), ROWS - 1)
                oc = jnp.minimum(jnp.maximum(c + dc, 0), COLS - 1)
                other = su[pl.ds(pl.multiple_of((oc * ROWS + o) * PIECES + RAW, 8), 8), :]
                values = src[rows_at((oc + 1) * ROWS + o, 8), :] * jnp.where(within, 1.0, 0.0)
                total = total + direct_total(own, other, values)
            totals[pl.ds(t, 8, stride=TILES), :] = total
            return carry

        lax.fori_loop(0, TILES, tile, 0)


def rim_body(
    coords, stiff, links, inside, x_first, x_second, y_first, y_second,
    damage, strength, peak,
    sv, sides, su, vt, vt_sides, block, block_sides, weights, src, raw, totals,
):
    before, after = facing(x_first, x_second, "gx")
    left, right = facing(y_first, y_second, "gy")
    f32, bf16 = jnp.float32, jnp.bfloat16
    gx, gy = lax.axis_index("gx"), lax.axis_index("gy")
    has_top, has_bot = gx > 0, gx < lax.axis_size("gx") - 1
    has_left, has_right = gy > 0, gy < lax.axis_size("gy") - 1
    other_const, own_const, ones = constant_rows()
    zero8 = jnp.zeros((8, PTS), f32)
    totals[...] = inside[...]
    for c in range(EXT_COLS):
        for h in range(2):
            sv[pl.ds(c * PTS + h * PIECES + 16, 8), :] = other_const
            sv[pl.ds(c * PTS + h * PIECES + 24, 8), :] = zero8
            src[pl.ds(((h * LAST) * EXT_COLS + c) * 8, 8), :] = ones
        sv[pl.ds(c * PTS + 64, 64), :] = jnp.zeros((64, PTS), f32)
    for r in range(ROWS):
        for h in range(2):
            sides[pl.ds((h * ROWS + r) * PIECES + 16, 8), :] = other_const
            sides[pl.ds((h * ROWS + r) * PIECES + 24, 8), :] = zero8
            src[pl.ds(((r + 1) * EXT_COLS + h * (EXT_COLS - 1)) * 8, 8), :] = ones
    for t in range(TILES):
        su[pl.ds(t * PIECES + 16, 8), :] = own_const
        su[pl.ds(t * PIECES + 24, 8), :] = zero8
    block[...] = jnp.zeros(block.shape, bf16)
    block_sides[...] = jnp.zeros(block_sides.shape, bf16)

    centre = centre_of(coords)
    far = jnp.zeros((COLS, PTS), f32)
    for r in range(ROWS):
        xyz = [coords[x, r] for x in range(3)]
        a, norm = scaled(xyz, centre)
        far = jnp.maximum(far, norm)
        put_own(su, a, norm, xyz, lambda k: pl.ds(r * PIECES + k, COLS, stride=ROWS * PIECES))
    for h, halo, there in ((0, before, has_top), (1, after, has_bot)):
        xyz = [halo(x) for x in range(3)]
        a, norm = scaled(xyz, centre)
        far = jnp.maximum(far, jnp.where(there, norm, 0.0))
        put_other(sv, a, norm, lambda k: pl.ds(PTS + h * PIECES + k, COLS, stride=PTS))
        first = (h * LAST * EXT_COLS + 1) * 8
        for x in range(3):
            raw[pl.ds(first + x, COLS, stride=8), :] = xyz[x]
        for l in range(LAYERS):
            src[pl.ds(first + l, COLS, stride=8), :] = halo(3 + l)
    rows6 = lax.broadcasted_iota(jnp.int32, (EXT_ROWS, PTS), 0)
    there6 = ((rows6 > 0) | has_top) & ((rows6 < LAST) | has_bot)
    side = jnp.zeros((EXT_ROWS, PTS), f32)
    for h, halo, there in ((0, left, has_left), (1, right, has_right)):
        xyz = [halo(x) for x in range(3)]
        a, norm = scaled(xyz, centre)
        side = jnp.maximum(side, jnp.where(there6 & there, norm, 0.0))
        mid = [v[1:LAST] for v in a]
        put_other(sides, mid, norm[1:LAST], lambda k: pl.ds(h * ROWS * PIECES + k, ROWS, stride=PIECES))
        col = h * (EXT_COLS - 1)
        for e in range(2):
            one = slice(e * LAST, e * LAST + 1)
            put_other(sv, [v[one] for v in a], norm[one], lambda k: pl.ds(col * PTS + e * PIECES + k, 1))
        for x in range(3):
            raw[pl.ds(col * 8 + x, EXT_ROWS, stride=EXT_COLS * 8), :] = xyz[x]
        for l in range(LAYERS):
            src[pl.ds(col * 8 + l, EXT_ROWS, stride=EXT_COLS * 8), :] = halo(3 + l)
    near = jnp.maximum(jnp.max(far), jnp.max(side)) <= SPREAD_LIMIT

    def add(r, c, value):
        at = pl.ds(r * COLS + c, 8, stride=TILES)
        totals[at, :] = totals[at, :] + value

    @pl.when(near)
    def _():
        def turn(c, carry):
            vt[rows_at(c, PTS), :] = sv[rows_at(c, PTS), :].T.astype(bf16)
            return carry

        lax.fori_loop(0, EXT_COLS, turn, 0, unroll=9)
        vt_sides[...] = sides[...].T.astype(bf16)
        for h in range(2):
            for j, (o, r) in enumerate(INSIDE):
                own = su[pl.ds((h * (COLS - 1) * ROWS + r) * PIECES, PIECES), :].astype(bf16)
                block_sides[pl.ds((h * ROWS + o) * PIECES, PIECES), pl.ds((h * len(INSIDE) + j) * PTS, PTS)] = own
        for j in range(0, 2 * len(INSIDE), 2):
            weights[pl.ds(3 * PTS * COLS + (j // 2) * PTS, PTS), :] = bell_weights(
                vt_sides[...], block_sides[:, j * PTS : (j + 2) * PTS]
            )

        def weigh(c, carry):
            for h in range(2):
                own = su[rows_at(c * ROWS + h * (ROWS - 1), PIECES), :].astype(bf16)
                block[rows_at(2 * c + h, PIECES), pl.ds(h * PTS, PTS)] = own
            here = block[rows_at(c, 2 * PIECES), :]
            own = jnp.concatenate([here, jnp.zeros((64, 2 * PTS), bf16)], axis=0)
            weights[rows_at(c, 3 * PTS), :] = bell_weights(vt[rows_at(c, PTS, 3 * PTS), :], own)
            return carry

        lax.fori_loop(0, COLS, weigh, 0, unroll=4)

        def total(c, carry):
            halves = []
            for h in range(2):
                parts = [
                    src[rows_at(h * LAST * EXT_COLS + c + dc, 8), :] * is_live(links, 2 * h - 1, dc - 1, h * (ROWS - 1), c)
                    for dc in range(3)
                ]
                halves.append(jnp.concatenate(parts, axis=1))
            values = jnp.concatenate(halves, axis=0).astype(bf16)
            out = jnp.dot(values, weights[rows_at(c, 3 * PTS), :], preferred_element_type=f32)
            for h in range(2):
                add(h * (ROWS - 1), c, out[8 * h : 8 * h + 8, h * PTS : (h + 1) * PTS])
            return carry

        lax.fori_loop(0, COLS, total, 0, unroll=4)
        sums = [[zero8 for _ in range(ROWS)] for _ in range(2)]
        for j in range(0, 2 * len(INSIDE), 2):
            halves, owners = [], []
            for i in (j, j + 1):
                h, (o, r) = i // len(INSIDE), INSIDE[i % len(INSIDE)]
                held = src[pl.ds(((o + 1) * EXT_COLS + h * (EXT_COLS - 1)) * 8, 8), :]
                halves.append(held * is_live(links, o - r, 2 * h - 1, r, h * (COLS - 1)))
                owners.append((h, r))
            values = jnp.concatenate(halves, axis=0).astype(bf16)
            pair = weights[pl.ds(3 * PTS * COLS + (j // 2) * PTS, PTS), :]
            out = jnp.dot(values, pair, preferred_element_type=f32)
            for i, (h, r) in enumerate(owners):
                sums[h][r] = sums[h][r] + out[8 * i : 8 * i + 8, i * PTS : (i + 1) * PTS]
        for h in range(2):
            for r in range(ROWS):
                add(r, h * (COLS - 1), sums[h][r])

    @pl.when(jnp.logical_not(near))
    def _():
        def tile(t, carry):
            r, c = t // COLS, t % COLS
            own = su[pl.ds(pl.multiple_of((c * ROWS + r) * PIECES + RAW, 8), 8), :]
            for (dr, dc), slot in SLOT_OF.items():
                o, oc = r + dr, c + dc
                within = (o >= 0) & (o < ROWS) & (oc >= 0) & (oc < COLS)

                @pl.when(jnp.logical_not(within) & (links[slot, r, c] >= 0))
                def _():
                    at = rows_at((o + 1) * EXT_COLS + oc + 1, 8)
                    add(r, c, direct_total(own, raw[at, :], src[at, :]))

            return carry

        lax.fori_loop(0, TILES, tile, 0)

    for r in range(ROWS):
        weight_sum = totals[pl.ds(LAYERS * TILES + r * COLS, COLS), :]
        mean = jnp.zeros((COLS, PTS), f32)
        for l in range(LAYERS):
            averaged = totals[pl.ds(l * TILES + r * COLS, COLS), :] / weight_sum
            value = averaged / (averaged + STRAIN_SCALE)
            damage[l, r] = value
            mean = mean + value
        power = (1.0 - mean / LAYERS) * stiff[0, r]
        strength[r] = power
        top = jnp.maximum(top, power) if r else power
    peak[...] = jnp.full(peak.shape, jnp.max(top), f32)


def force_body(
    disp, strength, corners, x_first, x_second, y_first, y_second,
    inner, rim_first, rim_second, rim_left, rim_right,
    edisp, amounts, forces,
):
    f32, bf16 = jnp.float32, jnp.bfloat16
    before, after = facing(x_first, x_second, "gx")
    left, right = facing(y_first, y_second, "gy")
    even = lax.axis_index("gx") % 2 == 0
    forces[...] = jnp.zeros(forces.shape, f32)
    for x in range(3):
        for r in range(EXT_ROWS):
            row = before(8 + x) if r == 0 else after(8 + x) if r == LAST else disp[x, r - 1]
            edisp[pl.ds((x * EXT_ROWS + r) * DISP_COLS + 1, COLS), :] = row
        edisp[pl.ds(x * EXT_ROWS * DISP_COLS, EXT_ROWS, stride=DISP_COLS), :] = left(8 + x)
        edisp[pl.ds(x * EXT_ROWS * DISP_COLS + COLS + 1, EXT_ROWS, stride=DISP_COLS), :] = right(8 + x)

    def gather(r, carry):
        for g in range(COLS // 8):
            power = strength[r, 8 * g : 8 * g + 8, :]
            codes = [corners[k, r, 8 * g : 8 * g + 8, :] for k in range(4)]
            offset = [code >> 7 for code in codes]
            slot = [code & (PTS - 1) for code in codes]
            at = [
                pl.ds(pl.multiple_of(((r * COLS + 8 * g) * 4 + k) * 8, 8) + i, 8, stride=32)
                for k in range(4) for i in range(8)
            ]
            for k in range(4):
                amounts[at[8 * k + 3], :] = offset[k].astype(f32)
                amounts[at[8 * k + 7], :] = slot[k].astype(f32)
            for x in range(3):
                picked = []
                base = (x * EXT_ROWS + r) * DISP_COLS + 8 * g
                table = [edisp[pl.ds(base + (o // 3) * DISP_COLS + o % 3, 8), :] for o in range(9)]
                for k in range(4):
                    found = jnp.take_along_axis(table[0], slot[k], axis=1)
                    for o in range(1, 9):
                        found = jnp.where(offset[k] == o, jnp.take_along_axis(table[o], slot[k], axis=1), found)
                    picked.append(found)
                springs = [power * (picked[(k + 1) % 4] - picked[k]) for k in range(4)]
                for k in range(4):
                    amount = springs[k] - springs[(k + 3) % 4]
                    hi = amount.astype(bf16).astype(f32)
                    amounts[at[8 * k + x], :] = hi
                    amounts[at[8 * k + 4 + x], :] = amount - hi
        return carry

    lax.fori_loop(0, ROWS, gather, 0, unroll=2)

    nodes = lax.broadcasted_iota(jnp.int32, (PTS, PTS), 0).astype(f32)

    def scatter(t, carry):
        r, c = t // COLS, t % COLS
        picks, rows = [], []
        for k in range(4):
            own = amounts[pl.ds(pl.multiple_of((t * 4 + k) * 8, 8), 8), :]
            offset, slot = own[3:4, :], own[7:8, :]
            rows.append(jnp.concatenate([jnp.where(offset == float(o), own, 0.0) for o in range(10)], axis=0))
            picks.append(jnp.where(slot == nodes, 1.0, 0.0).astype(bf16))
        left_side = jnp.concatenate(rows, axis=1).astype(bf16)
        right_side = jnp.concatenate(picks, axis=1)
        out = lax.dot_general(left_side, right_side, (((1,), (1,)), ((), ())), preferred_element_type=f32)
        for o in range(9):
            at = pl.ds(pl.multiple_of(((r + o // 3) * EXT_COLS + c + o % 3) * 8, 8), 8)
            forces[at, :] = forces[at, :] + out[8 * o : 8 * o + 8]
        return carry

    lax.fori_loop(0, ROWS * COLS, scatter, 0, unroll=8)

    def node_sum(x, first, count, stride):
        return (
            forces[pl.ds(first * 8 + x, count, stride=8 * stride), :]
            + forces[pl.ds(first * 8 + 4 + x, count, stride=8 * stride), :]
        )

    for x in range(3):
        for r in range(ROWS):
            inner[x, r] = node_sum(x, (r + 1) * EXT_COLS + 1, COLS, 1)
        top = node_sum(x, 0, EXT_COLS, 1)
        bottom = node_sum(x, LAST * EXT_COLS, EXT_COLS, 1)
        rim_first[x] = jnp.where(even, bottom, top)
        rim_second[x] = jnp.where(even, top, bottom)
        rim_left[x] = node_sum(x, EXT_COLS, ROWS, EXT_COLS)
        rim_right[x] = node_sum(x, 2 * EXT_COLS - 1, ROWS, EXT_COLS)


def finish_body(inner, x_first, x_second, y_first, y_second, peaks, out):
    before, after = facing(x_first, x_second, "gx")
    left, right = facing(y_first, y_second, "gy")
    top = jnp.max(peaks[...])
    cols = lax.broadcasted_iota(jnp.int32, (COLS, PTS), 0)
    for x in range(3):
        west, east = left(x), right(x)
        for r in range(ROWS):
            value = inner[x, r]
            if r == 0:
                value = value + before(x)[1 : COLS + 1]
            if r == ROWS - 1:
                value = value + after(x)[1 : COLS + 1]
            value = value + jnp.where(cols == 0, west[r : r + 1], 0.0) + jnp.where(cols == COLS - 1, east[r : r + 1], 0.0)
            out[x, r] = value / top


def kernels(peers):
    f32, bf16 = jnp.float32, jnp.bfloat16
    vmem = pl.BlockSpec(memory_space=pltpu.VMEM)
    smem = pl.BlockSpec(memory_space=pltpu.SMEM)

    def call(body, name, ins, outs, scratch, flops):
        return pl.pallas_call(
            body,
            out_shape=tuple(jax.ShapeDtypeStruct(*o) for o in outs),
            in_specs=[smem if i == "links" else vmem for i in ins],
            out_specs=(vmem,) * len(outs),
            scratch_shapes=[pltpu.VMEM(*v) for v in scratch],
            compiler_params=pltpu.CompilerParams(vmem_limit_bytes=40 * MIB),
            cost_estimate=pl.CostEstimate(flops=flops, bytes_accessed=MIB, transcendentals=0),
            name=name,
        )

    inside = call(
        inside_body,
        "inside_links",
        ("strain", "coords", "links"),
        [((8 * TILES, PTS), f32)],
        [
            ((TILES * PIECES, PTS), f32),
            ((TILES * PIECES, PTS), f32),
            ((EXT_COLS * PTS, PTS), bf16),
            ((PTS, len(INSIDE) * PTS), bf16),
            ((3 * PTS, len(INSIDE) * PTS), bf16),
            ((EXT_COLS * ROWS * 8, PTS), f32),
        ],
        8 * 10**9,
    )
    rim = call(
        rim_body,
        "rim_links",
        ("coords", "stiff", "links", "inside", "x_first", "x_second", "y_first", "y_second"),
        [((LAYERS, ROWS, COLS, PTS), f32), ((ROWS, COLS, PTS), f32), ((peers, PTS), f32)],
        [
            ((EXT_COLS * PTS, PTS), f32),
            ((2 * PTS, PTS), f32),
            ((TILES * PIECES, PTS), f32),
            ((EXT_COLS * PTS, PTS), bf16),
            ((PTS, 2 * PTS), bf16),
            ((COLS * 2 * PIECES, 2 * PTS), bf16),
            ((2 * PTS, 2 * len(INSIDE) * PTS), bf16),
            ((3 * PTS * COLS + len(INSIDE) * PTS, 2 * PTS), bf16),
            ((EXT_ROWS * EXT_COLS * 8, PTS), f32),
            ((EXT_ROWS * EXT_COLS * 8, PTS), f32),
            ((8 * TILES, PTS), f32),
        ],
        4 * 10**9,
    )
    force = call(
        force_body,
        "node_forces",
        ("disp", "strength", "corners", "x_first", "x_second", "y_first", "y_second"),
        [
            ((3, ROWS, COLS, PTS), f32),
            ((3, EXT_COLS, PTS), f32),
            ((3, EXT_COLS, PTS), f32),
            ((3, ROWS, PTS), f32),
            ((3, ROWS, PTS), f32),
        ],
        [
            ((3 * EXT_ROWS * DISP_COLS, PTS), f32),
            ((TILES * 32, PTS), f32),
            ((EXT_ROWS * EXT_COLS * 8, PTS), f32),
        ],
        8 * 10**9,
    )
    finish = call(
        finish_body,
        "finish",
        ("inner", "x_first", "x_second", "y_first", "y_second", "peaks"),
        [((3, ROWS, COLS, PTS), f32)],
        [],
        10**6,
    )
    return inside, rim, force, finish


def swap(first, second, axis):
    peers = lax.axis_size(axis)
    with_first = [(i, i ^ 1) for i in range(peers)]
    with_second = [(i, ((i - 1) ^ 1) + 1) for i in range(1, peers - 1)]
    return lax.ppermute(first, axis, with_first), lax.ppermute(second, axis, with_second)


def local(strain, coords, displacement, stiffness, neighbours, corners):
    peers_x, peers_y = lax.axis_size("gx"), lax.axis_size("gy")
    even_x, even_y = lax.axis_index("gx") % 2 == 0, lax.axis_index("gy") % 2 == 0
    own = (coords, strain, displacement)

    def take(value, index, dim):
        return lax.dynamic_index_in_dim(value, index, dim, keepdims=False)

    def row(r):
        return jnp.concatenate([take(v, r, 1) for v in own], axis=0)

    inside, rim, force, finish = kernels(peers_x)
    x_halos = swap(row(jnp.where(even_x, ROWS - 1, 0)), row(jnp.where(even_x, 0, ROWS - 1)), "gx")
    above = jnp.where(even_x, x_halos[1], x_halos[0])
    below = jnp.where(even_x, x_halos[0], x_halos[1])

    def column(c):
        mid = jnp.concatenate([take(v, c, 2) for v in own], axis=0)
        return jnp.concatenate([take(above, c, 1)[:, None], mid, take(below, c, 1)[:, None]], axis=1)

    y_halos = swap(column(jnp.where(even_y, COLS - 1, 0)), column(jnp.where(even_y, 0, COLS - 1)), "gy")
    totals = inside(strain, coords, neighbours)[0]
    damage, strength, peak = rim(coords, stiffness, neighbours, totals, *x_halos, *y_halos)
    peaks = lax.all_to_all(peak, "gx", 0, 0, tiled=True)
    inner, rim_first, rim_second, rim_left, rim_right = force(displacement, strength, corners, *x_halos, *y_halos)
    x_rims = swap(rim_first, rim_second, "gx")
    *x_rims, peaks = lax.optimization_barrier((*x_rims, peaks))
    peaks = jnp.broadcast_to(jnp.max(peaks, axis=0, keepdims=True), (peers_y, PTS))
    peaks = lax.all_to_all(peaks, "gy", 0, 0, tiled=True)
    above = jnp.where(even_x, x_rims[1], x_rims[0])
    below = jnp.where(even_x, x_rims[0], x_rims[1])

    def side(rim_side, c):
        return rim_side.at[:, 0].add(above[:, c]).at[:, ROWS - 1].add(below[:, c])

    west, east = side(rim_left, 0), side(rim_right, EXT_COLS - 1)
    y_rims = swap(jnp.where(even_y, east, west), jnp.where(even_y, west, east), "gy")
    return damage, finish(inner, *x_rims, *y_rims, peaks)[0]


def solution(mesh):
    spec = P(None, "gx", "gy", None)
    in_specs = (spec, spec, spec, spec, P(None, "gx", "gy"), spec)
    return jax.shard_map(local, mesh=mesh, in_specs=in_specs, out_specs=(spec, spec), check_vma=False)
```

```python
import jax
import jax.numpy as jnp
from jax import lax
from jax.experimental import pallas as pl
from jax.experimental.pallas import tpu as pltpu
from jax.sharding import PartitionSpec as P

PTS = 128
LAYERS = 5
ROWS = 4
COLS = 16
EXT_ROWS = ROWS + 2
LAST = ROWS + 1
EXT_COLS = COLS + 2
STRAIN_SCALE = 0.05
INV_RADIUS = 0.1
SPREAD_LIMIT = 128.0
SLOT_OF = {(0, 0): 0, (-1, -1): 1, (-1, 0): 2, (-1, 1): 3, (0, -1): 4, (0, 1): 5, (1, -1): 6, (1, 0): 7, (1, 1): 8}
PIECES = 32
RAW = 24
TILES = ROWS * COLS
DISP_COLS = 24
INSIDE = [(o, r) for r in range(ROWS) for o in range(ROWS) if abs(o - r) <= 1]
V_ROWS = (0, 3, 6, 9, 12, 15)
MIB = 1024 * 1024


def split3(value):
    hi = value.astype(jnp.bfloat16).astype(jnp.float32)
    rest = value - hi
    mid = rest.astype(jnp.bfloat16).astype(jnp.float32)
    return hi, mid, rest - mid


def scaled(xyz, centre):
    a = [(xyz[x] - centre[x]) * INV_RADIUS for x in range(3)]
    return a, a[0] * a[0] + a[1] * a[1] + a[2] * a[2]


def centre_of(coords):
    return [0.5 * (jnp.min(coords[x]) + jnp.max(coords[x])) for x in range(3)]


def put_other(sv, a, norm, at):
    for x in range(3):
        hi, mid, lo = split3(a[x])
        for k, v in zip(V_ROWS, (hi, hi, mid, mid, hi, lo)):
            sv[at(k + x), :] = v
    for k, v in enumerate(split3(-norm)):
        sv[at(21 + k), :] = v


def put_own(su, a, norm, xyz, at):
    for x in range(3):
        hi, mid, lo = split3(a[x])
        for k, v in zip(V_ROWS, (hi, mid, hi, mid, lo, hi)):
            su[at(k + x), :] = 2.0 * v
        su[at(RAW + x), :] = xyz[x]
    for k, v in enumerate(split3(1.0 - norm)):
        su[at(18 + k), :] = v


def constant_rows():
    row8 = lax.broadcasted_iota(jnp.int32, (8, PTS), 0)
    other = jnp.where((row8 >= 2) & (row8 <= 4), 1.0, 0.0)
    own = jnp.where(row8 >= 5, 1.0, 0.0)
    ones = jnp.where(row8 == LAYERS, 1.0, 0.0)
    return other.astype(jnp.float32), own.astype(jnp.float32), ones.astype(jnp.float32)


def rows_at(index, size, count=None):
    return pl.ds(pl.multiple_of(index * size, size), size if count is None else count)


def bell_weights(other, own):
    bell = jnp.maximum(jnp.dot(other, own, preferred_element_type=jnp.float32), 0.0)
    return (bell * bell).astype(jnp.bfloat16)


def direct_total(own, other, values):
    turned = jnp.concatenate([other] + [jnp.zeros((8, PTS), jnp.float32)] * 15, axis=0).T
    dist = jnp.zeros((PTS, PTS), jnp.float32)
    for x in range(3):
        dist = dist + (own[x : x + 1, :] - turned[:, x : x + 1]) ** 2
    bell = jnp.maximum(1.0 - dist * 0.01, 0.0)
    pair = (bell * bell).astype(jnp.bfloat16)
    return jnp.dot(values.astype(jnp.bfloat16), pair, preferred_element_type=jnp.float32)


def is_live(links, dr, dc, r, c):
    return jnp.where(links[SLOT_OF[(dr, dc)], r, c] >= 0, 1.0, 0.0).astype(jnp.float32)


def facing(first, second, axis):
    even = lax.axis_index(axis) % 2 == 0
    return (lambda i: jnp.where(even, second[i], first[i])), (lambda i: jnp.where(even, first[i], second[i]))


def split_body(strain, coords, su, vt, src, info, sv):
    f32, bf16 = jnp.float32, jnp.bfloat16
    other_const, own_const, ones = constant_rows()
    zero8 = jnp.zeros((8, PTS), f32)
    for c in range(EXT_COLS):
        edge = c in (0, EXT_COLS - 1)
        for r in range(ROWS):
            src[pl.ds((c * ROWS + r) * 8, 8), :] = zero8 if edge else ones
            if not edge:
                sv[pl.ds(((c - 1) * ROWS + r) * PIECES + 16, 8), :] = other_const
                sv[pl.ds(((c - 1) * ROWS + r) * PIECES + 24, 8), :] = zero8
    for t in range(TILES):
        su[pl.ds(t * PIECES + 16, 8), :] = own_const
        su[pl.ds(t * PIECES + 24, 8), :] = zero8
    for c in (0, EXT_COLS - 1):
        vt[pl.ds(c * PTS, PTS), :] = jnp.zeros((PTS, PTS), bf16)

    centre = centre_of(coords)
    far = jnp.zeros((COLS, PTS), f32)
    step = ROWS * PIECES
    for r in range(ROWS):
        xyz = [coords[x, r] for x in range(3)]
        a, norm = scaled(xyz, centre)
        far = jnp.maximum(far, norm)
        put_other(sv, a, norm, lambda k: pl.ds(r * PIECES + k, COLS, stride=step))
        put_own(su, a, norm, xyz, lambda k: pl.ds(r * PIECES + k, COLS, stride=step))
        for l in range(LAYERS):
            src[pl.ds((ROWS + r) * 8 + l, COLS, stride=ROWS * 8), :] = strain[l, r]
    info[...] = jnp.zeros(info.shape, f32)
    for x in range(3):
        info[x : x + 1] = jnp.full((1, PTS), centre[x], f32)
    info[3:4] = jnp.max(far, axis=0, keepdims=True)

    def turn(c, carry):
        vt[rows_at(c + 1, PTS), :] = sv[rows_at(c, step), :].T.astype(bf16)
        return carry

    lax.fori_loop(0, COLS, turn, 0, unroll=8)


def inside_body(links, su, vt, src, info, totals, block, weights):
    f32, bf16 = jnp.float32, jnp.bfloat16
    zero8 = jnp.zeros((8, PTS), f32)
    block[...] = jnp.zeros(block.shape, bf16)
    near = jnp.max(info[3:4]) <= SPREAD_LIMIT

    @pl.when(near)
    def _():
        def column(c, carry):
            for j, (o, r) in enumerate(INSIDE):
                own = su[rows_at(c * ROWS + r, PIECES), :]
                block[pl.ds(o * PIECES, PIECES), pl.ds(j * PTS, PTS)] = own.astype(bf16)
            others = vt[rows_at(c, PTS, 3 * PTS), :]
            for j in range(0, len(INSIDE), 2):
                weights[:, j * PTS : (j + 2) * PTS] = bell_weights(others, block[:, j * PTS : (j + 2) * PTS])
            sums = [zero8 for _ in range(ROWS)]
            for j in range(0, len(INSIDE), 2):
                halves = []
                for o, r in INSIDE[j : j + 2]:
                    parts = [src[rows_at((c + dc) * ROWS + o, 8), :] * is_live(links, o - r, dc - 1, r, c) for dc in range(3)]
                    halves.append(jnp.concatenate(parts, axis=1))
                values = jnp.concatenate(halves, axis=0).astype(bf16)
                out = jnp.dot(values, weights[:, j * PTS : (j + 2) * PTS], preferred_element_type=f32)
                for h in range(2):
                    r = INSIDE[j + h][1]
                    sums[r] = sums[r] + out[8 * h : 8 * h + 8, h * PTS : (h + 1) * PTS]
            for r in range(ROWS):
                totals[pl.ds(r * COLS + c, 8, stride=TILES), :] = sums[r]
            return carry

        lax.fori_loop(0, COLS, column, 0, unroll=4)

    @pl.when(jnp.logical_not(near))
    def _():
        def tile(t, carry):
            r, c = t // COLS, t % COLS
            own = su[pl.ds(pl.multiple_of((c * ROWS + r) * PIECES + RAW, 8), 8), :]
            total = zero8
            for (dr, dc), slot in SLOT_OF.items():
                within = (r + dr >= 0) & (r + dr < ROWS) & (c + dc >= 0) & (c + dc < COLS) & (links[slot, r, c] >= 0)
                o = jnp.minimum(jnp.maximum(r + dr, 0), ROWS - 1)
                oc = jnp.minimum(jnp.maximum(c + dc, 0), COLS - 1)
                other = su[pl.ds(pl.multiple_of((oc * ROWS + o) * PIECES + RAW, 8), 8), :]
                values = src[rows_at((oc + 1) * ROWS + o, 8), :] * jnp.where(within, 1.0, 0.0)
                total = total + direct_total(own, other, values)
            totals[pl.ds(t, 8, stride=TILES), :] = total
            return carry

        lax.fori_loop(0, TILES, tile, 0)


def rim_body(
    stiff, links, inside, su, info, x_first, x_second, y_first, y_second,
    damage, strength, peak,
    sv, sides, vt, vt_sides, block, block_sides, weights, src, raw, totals,
):
    before, after = facing(x_first, x_second, "gx")
    left, right = facing(y_first, y_second, "gy")
    f32, bf16 = jnp.float32, jnp.bfloat16
    gx, gy = lax.axis_index("gx"), lax.axis_index("gy")
    has_top, has_bot = gx > 0, gx < lax.axis_size("gx") - 1
    has_left, has_right = gy > 0, gy < lax.axis_size("gy") - 1
    other_const, _, ones = constant_rows()
    zero8 = jnp.zeros((8, PTS), f32)
    totals[...] = inside[...]
    for c in range(EXT_COLS):
        for h in range(2):
            sv[pl.ds(c * PTS + h * PIECES + 16, 8), :] = other_const
            sv[pl.ds(c * PTS + h * PIECES + 24, 8), :] = zero8
            src[pl.ds(((h * LAST) * EXT_COLS + c) * 8, 8), :] = ones
        sv[pl.ds(c * PTS + 64, 64), :] = jnp.zeros((64, PTS), f32)
    for r in range(ROWS):
        for h in range(2):
            sides[pl.ds((h * ROWS + r) * PIECES + 16, 8), :] = other_const
            sides[pl.ds((h * ROWS + r) * PIECES + 24, 8), :] = zero8
            src[pl.ds(((r + 1) * EXT_COLS + h * (EXT_COLS - 1)) * 8, 8), :] = ones
    block[...] = jnp.zeros(block.shape, bf16)
    block_sides[...] = jnp.zeros(block_sides.shape, bf16)

    centre = [info[x : x + 1, :] for x in range(3)]
    far = jnp.broadcast_to(info[3:4, :], (COLS, PTS))
    for h, halo, there in ((0, before, has_top), (1, after, has_bot)):
        xyz = [halo(x) for x in range(3)]
        a, norm = scaled(xyz, centre)
        far = jnp.maximum(far, jnp.where(there, norm, 0.0))
        put_other(sv, a, norm, lambda k: pl.ds(PTS + h * PIECES + k, COLS, stride=PTS))
        first = (h * LAST * EXT_COLS + 1) * 8
        for x in range(3):
            raw[pl.ds(first + x, COLS, stride=8), :] = xyz[x]
        for l in range(LAYERS):
            src[pl.ds(first + l, COLS, stride=8), :] = halo(3 + l)
    rows6 = lax.broadcasted_iota(jnp.int32, (EXT_ROWS, PTS), 0)
    there6 = ((rows6 > 0) | has_top) & ((rows6 < LAST) | has_bot)
    side = jnp.zeros((EXT_ROWS, PTS), f32)
    for h, halo, there in ((0, left, has_left), (1, right, has_right)):
        xyz = [halo(x) for x in range(3)]
        a, norm = scaled(xyz, centre)
        side = jnp.maximum(side, jnp.where(there6 & there, norm, 0.0))
        mid = [v[1:LAST] for v in a]
        put_other(sides, mid, norm[1:LAST], lambda k: pl.ds(h * ROWS * PIECES + k, ROWS, stride=PIECES))
        col = h * (EXT_COLS - 1)
        for e in range(2):
            one = slice(e * LAST, e * LAST + 1)
            put_other(sv, [v[one] for v in a], norm[one], lambda k: pl.ds(col * PTS + e * PIECES + k, 1))
        for x in range(3):
            raw[pl.ds(col * 8 + x, EXT_ROWS, stride=EXT_COLS * 8), :] = xyz[x]
        for l in range(LAYERS):
            src[pl.ds(col * 8 + l, EXT_ROWS, stride=EXT_COLS * 8), :] = halo(3 + l)
    near = jnp.maximum(jnp.max(far), jnp.max(side)) <= SPREAD_LIMIT

    def add(r, c, value):
        at = pl.ds(r * COLS + c, 8, stride=TILES)
        totals[at, :] = totals[at, :] + value

    @pl.when(near)
    def _():
        def turn(c, carry):
            vt[rows_at(c, PTS), :] = sv[rows_at(c, PTS), :].T.astype(bf16)
            return carry

        lax.fori_loop(0, EXT_COLS, turn, 0, unroll=9)
        vt_sides[...] = sides[...].T.astype(bf16)
        for h in range(2):
            for j, (o, r) in enumerate(INSIDE):
                own = su[pl.ds((h * (COLS - 1) * ROWS + r) * PIECES, PIECES), :].astype(bf16)
                block_sides[pl.ds((h * ROWS + o) * PIECES, PIECES), pl.ds((h * len(INSIDE) + j) * PTS, PTS)] = own
        for j in range(0, 2 * len(INSIDE), 2):
            weights[pl.ds(3 * PTS * COLS + (j // 2) * PTS, PTS), :] = bell_weights(
                vt_sides[...], block_sides[:, j * PTS : (j + 2) * PTS]
            )

        def weigh(c, carry):
            for h in range(2):
                own = su[rows_at(c * ROWS + h * (ROWS - 1), PIECES), :].astype(bf16)
                block[rows_at(2 * c + h, PIECES), pl.ds(h * PTS, PTS)] = own
            here = block[rows_at(c, 2 * PIECES), :]
            own = jnp.concatenate([here, jnp.zeros((64, 2 * PTS), bf16)], axis=0)
            weights[rows_at(c, 3 * PTS), :] = bell_weights(vt[rows_at(c, PTS, 3 * PTS), :], own)
            return carry

        lax.fori_loop(0, COLS, weigh, 0, unroll=4)

        def total(c, carry):
            halves = []
            for h in range(2):
                parts = [
                    src[rows_at(h * LAST * EXT_COLS + c + dc, 8), :] * is_live(links, 2 * h - 1, dc - 1, h * (ROWS - 1), c)
                    for dc in range(3)
                ]
                halves.append(jnp.concatenate(parts, axis=1))
            values = jnp.concatenate(halves, axis=0).astype(bf16)
            out = jnp.dot(values, weights[rows_at(c, 3 * PTS), :], preferred_element_type=f32)
            for h in range(2):
                add(h * (ROWS - 1), c, out[8 * h : 8 * h + 8, h * PTS : (h + 1) * PTS])
            return carry

        lax.fori_loop(0, COLS, total, 0, unroll=4)
        sums = [[zero8 for _ in range(ROWS)] for _ in range(2)]
        for j in range(0, 2 * len(INSIDE), 2):
            halves, owners = [], []
            for i in (j, j + 1):
                h, (o, r) = i // len(INSIDE), INSIDE[i % len(INSIDE)]
                held = src[pl.ds(((o + 1) * EXT_COLS + h * (EXT_COLS - 1)) * 8, 8), :]
                halves.append(held * is_live(links, o - r, 2 * h - 1, r, h * (COLS - 1)))
                owners.append((h, r))
            values = jnp.concatenate(halves, axis=0).astype(bf16)
            pair = weights[pl.ds(3 * PTS * COLS + (j // 2) * PTS, PTS), :]
            out = jnp.dot(values, pair, preferred_element_type=f32)
            for i, (h, r) in enumerate(owners):
                sums[h][r] = sums[h][r] + out[8 * i : 8 * i + 8, i * PTS : (i + 1) * PTS]
        for h in range(2):
            for r in range(ROWS):
                add(r, h * (COLS - 1), sums[h][r])

    @pl.when(jnp.logical_not(near))
    def _():
        def tile(t, carry):
            r, c = t // COLS, t % COLS
            own = su[pl.ds(pl.multiple_of((c * ROWS + r) * PIECES + RAW, 8), 8), :]
            for (dr, dc), slot in SLOT_OF.items():
                o, oc = r + dr, c + dc
                within = (o >= 0) & (o < ROWS) & (oc >= 0) & (oc < COLS)

                @pl.when(jnp.logical_not(within) & (links[slot, r, c] >= 0))
                def _():
                    at = rows_at((o + 1) * EXT_COLS + oc + 1, 8)
                    add(r, c, direct_total(own, raw[at, :], src[at, :]))

            return carry

        lax.fori_loop(0, TILES, tile, 0)

    for r in range(ROWS):
        weight_sum = totals[pl.ds(LAYERS * TILES + r * COLS, COLS), :]
        mean = jnp.zeros((COLS, PTS), f32)
        for l in range(LAYERS):
            averaged = totals[pl.ds(l * TILES + r * COLS, COLS), :] / weight_sum
            value = averaged / (averaged + STRAIN_SCALE)
            damage[l, r] = value
            mean = mean + value
        power = (1.0 - mean / LAYERS) * stiff[0, r]
        strength[r] = power
        top = jnp.maximum(top, power) if r else power
    peak[...] = jnp.full(peak.shape, jnp.max(top), f32)


def force_body(
    disp, strength, corners, x_first, x_second, y_first, y_second,
    inner, rim_first, rim_second, rim_left, rim_right,
    edisp, amounts, forces,
):
    f32, bf16 = jnp.float32, jnp.bfloat16
    before, after = facing(x_first, x_second, "gx")
    left, right = facing(y_first, y_second, "gy")
    even = lax.axis_index("gx") % 2 == 0
    forces[...] = jnp.zeros(forces.shape, f32)
    for x in range(3):
        for r in range(EXT_ROWS):
            row = before(8 + x) if r == 0 else after(8 + x) if r == LAST else disp[x, r - 1]
            edisp[pl.ds((x * EXT_ROWS + r) * DISP_COLS + 1, COLS), :] = row
        edisp[pl.ds(x * EXT_ROWS * DISP_COLS, EXT_ROWS, stride=DISP_COLS), :] = left(8 + x)
        edisp[pl.ds(x * EXT_ROWS * DISP_COLS + COLS + 1, EXT_ROWS, stride=DISP_COLS), :] = right(8 + x)

    def gather(r, carry):
        for g in range(COLS // 8):
            power = strength[r, 8 * g : 8 * g + 8, :]
            codes = [corners[k, r, 8 * g : 8 * g + 8, :] for k in range(4)]
            offset = [code >> 7 for code in codes]
            slot = [code & (PTS - 1) for code in codes]
            at = [
                pl.ds(pl.multiple_of(((r * COLS + 8 * g) * 4 + k) * 8, 8) + i, 8, stride=32)
                for k in range(4) for i in range(8)
            ]
            for k in range(4):
                amounts[at[8 * k + 3], :] = offset[k].astype(f32)
                amounts[at[8 * k + 7], :] = slot[k].astype(f32)
            for x in range(3):
                picked = []
                base = (x * EXT_ROWS + r) * DISP_COLS + 8 * g
                table = [edisp[pl.ds(base + (o // 3) * DISP_COLS + o % 3, 8), :] for o in range(9)]
                for k in range(4):
                    found = jnp.take_along_axis(table[0], slot[k], axis=1)
                    for o in range(1, 9):
                        found = jnp.where(offset[k] == o, jnp.take_along_axis(table[o], slot[k], axis=1), found)
                    picked.append(found)
                springs = [power * (picked[(k + 1) % 4] - picked[k]) for k in range(4)]
                for k in range(4):
                    amount = springs[k] - springs[(k + 3) % 4]
                    hi = amount.astype(bf16).astype(f32)
                    amounts[at[8 * k + x], :] = hi
                    amounts[at[8 * k + 4 + x], :] = amount - hi
        return carry

    lax.fori_loop(0, ROWS, gather, 0, unroll=2)

    nodes = lax.broadcasted_iota(jnp.int32, (PTS, PTS), 0).astype(f32)

    def scatter(t, carry):
        r, c = t // COLS, t % COLS
        picks, rows = [], []
        for k in range(4):
            own = amounts[pl.ds(pl.multiple_of((t * 4 + k) * 8, 8), 8), :]
            offset, slot = own[3:4, :], own[7:8, :]
            rows.append(jnp.concatenate([jnp.where(offset == float(o), own, 0.0) for o in range(10)], axis=0))
            picks.append(jnp.where(slot == nodes, 1.0, 0.0).astype(bf16))
        left_side = jnp.concatenate(rows, axis=1).astype(bf16)
        right_side = jnp.concatenate(picks, axis=1)
        out = lax.dot_general(left_side, right_side, (((1,), (1,)), ((), ())), preferred_element_type=f32)
        for o in range(9):
            at = pl.ds(pl.multiple_of(((r + o // 3) * EXT_COLS + c + o % 3) * 8, 8), 8)
            forces[at, :] = forces[at, :] + out[8 * o : 8 * o + 8]
        return carry

    lax.fori_loop(0, ROWS * COLS, scatter, 0, unroll=16)

    def node_sum(x, first, count, stride):
        return (
            forces[pl.ds(first * 8 + x, count, stride=8 * stride), :]
            + forces[pl.ds(first * 8 + 4 + x, count, stride=8 * stride), :]
        )

    for x in range(3):
        for r in range(ROWS):
            inner[x, r] = node_sum(x, (r + 1) * EXT_COLS + 1, COLS, 1)
        top = node_sum(x, 0, EXT_COLS, 1)
        bottom = node_sum(x, LAST * EXT_COLS, EXT_COLS, 1)
        rim_first[x] = jnp.where(even, bottom, top)
        rim_second[x] = jnp.where(even, top, bottom)
        rim_left[x] = node_sum(x, EXT_COLS, ROWS, EXT_COLS)
        rim_right[x] = node_sum(x, 2 * EXT_COLS - 1, ROWS, EXT_COLS)


def finish_body(inner, x_first, x_second, y_first, y_second, peaks, out):
    before, after = facing(x_first, x_second, "gx")
    left, right = facing(y_first, y_second, "gy")
    top = jnp.max(peaks[...])
    cols = lax.broadcasted_iota(jnp.int32, (COLS, PTS), 0)
    for x in range(3):
        west, east = left(x), right(x)
        for r in range(ROWS):
            value = inner[x, r]
            if r == 0:
                value = value + before(x)[1 : COLS + 1]
            if r == ROWS - 1:
                value = value + after(x)[1 : COLS + 1]
            value = value + jnp.where(cols == 0, west[r : r + 1], 0.0) + jnp.where(cols == COLS - 1, east[r : r + 1], 0.0)
            out[x, r] = value / top


def kernels(peers):
    f32, bf16 = jnp.float32, jnp.bfloat16
    vmem = pl.BlockSpec(memory_space=pltpu.VMEM)
    smem = pl.BlockSpec(memory_space=pltpu.SMEM)

    def call(body, name, ins, outs, scratch, flops):
        return pl.pallas_call(
            body,
            out_shape=tuple(jax.ShapeDtypeStruct(*o) for o in outs),
            in_specs=[smem if i == "links" else vmem for i in ins],
            out_specs=(vmem,) * len(outs),
            scratch_shapes=[pltpu.VMEM(*v) for v in scratch],
            compiler_params=pltpu.CompilerParams(vmem_limit_bytes=24 * MIB),
            cost_estimate=pl.CostEstimate(flops=flops, bytes_accessed=MIB, transcendentals=0),
            name=name,
        )

    split = call(
        split_body,
        "split_block",
        ("strain", "coords"),
        [
            ((TILES * PIECES, PTS), f32),
            ((EXT_COLS * PTS, PTS), bf16),
            ((EXT_COLS * ROWS * 8, PTS), f32),
            ((8, PTS), f32),
        ],
        [((TILES * PIECES, PTS), f32)],
        3 * 10**9,
    )
    inside = call(
        inside_body,
        "inside_links",
        ("links", "su", "vt", "src", "info"),
        [((8 * TILES, PTS), f32)],
        [
            ((PTS, len(INSIDE) * PTS), bf16),
            ((3 * PTS, len(INSIDE) * PTS), bf16),
        ],
        6 * 10**9,
    )
    rim = call(
        rim_body,
        "rim_links",
        ("stiff", "links", "inside", "su", "info", "x_first", "x_second", "y_first", "y_second"),
        [((LAYERS, ROWS, COLS, PTS), f32), ((ROWS, COLS, PTS), f32), ((peers, PTS), f32)],
        [
            ((EXT_COLS * PTS, PTS), f32),
            ((2 * PTS, PTS), f32),
            ((EXT_COLS * PTS, PTS), bf16),
            ((PTS, 2 * PTS), bf16),
            ((COLS * 2 * PIECES, 2 * PTS), bf16),
            ((2 * PTS, 2 * len(INSIDE) * PTS), bf16),
            ((3 * PTS * COLS + len(INSIDE) * PTS, 2 * PTS), bf16),
            ((EXT_ROWS * EXT_COLS * 8, PTS), f32),
            ((EXT_ROWS * EXT_COLS * 8, PTS), f32),
            ((8 * TILES, PTS), f32),
        ],
        4 * 10**9,
    )
    force = call(
        force_body,
        "node_forces",
        ("disp", "strength", "corners", "x_first", "x_second", "y_first", "y_second"),
        [
            ((3, ROWS, COLS, PTS), f32),
            ((3, EXT_COLS, PTS), f32),
            ((3, EXT_COLS, PTS), f32),
            ((3, ROWS, PTS), f32),
            ((3, ROWS, PTS), f32),
        ],
        [
            ((3 * EXT_ROWS * DISP_COLS, PTS), f32),
            ((TILES * 32, PTS), f32),
            ((EXT_ROWS * EXT_COLS * 8, PTS), f32),
        ],
        8 * 10**9,
    )
    finish = call(
        finish_body,
        "finish",
        ("inner", "x_first", "x_second", "y_first", "y_second", "peaks"),
        [((3, ROWS, COLS, PTS), f32)],
        [],
        10**6,
    )
    return split, inside, rim, force, finish


def swap(first, second, axis):
    peers = lax.axis_size(axis)
    with_first = [(i, i ^ 1) for i in range(peers)]
    with_second = [(i, ((i - 1) ^ 1) + 1) for i in range(1, peers - 1)]
    return lax.ppermute(first, axis, with_first), lax.ppermute(second, axis, with_second)


def local(strain, coords, displacement, stiffness, neighbours, corners):
    peers_x, peers_y = lax.axis_size("gx"), lax.axis_size("gy")
    even_x, even_y = lax.axis_index("gx") % 2 == 0, lax.axis_index("gy") % 2 == 0
    own = (coords, strain, displacement)

    def take(value, index, dim):
        return lax.dynamic_index_in_dim(value, index, dim, keepdims=False)

    def row(r):
        return jnp.concatenate([take(v, r, 1) for v in own], axis=0)

    split, inside, rim, force, finish = kernels(peers_x)
    x_halos = swap(row(jnp.where(even_x, ROWS - 1, 0)), row(jnp.where(even_x, 0, ROWS - 1)), "gx")
    pieces = split(strain, coords)
    *x_halos, pieces = lax.optimization_barrier((*x_halos, pieces))
    above = jnp.where(even_x, x_halos[1], x_halos[0])
    below = jnp.where(even_x, x_halos[0], x_halos[1])

    def column(c):
        mid = jnp.concatenate([take(v, c, 2) for v in own], axis=0)
        return jnp.concatenate([take(above, c, 1)[:, None], mid, take(below, c, 1)[:, None]], axis=1)

    y_halos = swap(column(jnp.where(even_y, COLS - 1, 0)), column(jnp.where(even_y, 0, COLS - 1)), "gy")
    own_pieces, _, _, info = pieces
    totals = inside(neighbours, *pieces)[0]
    damage, strength, peak = rim(stiffness, neighbours, totals, own_pieces, info, *x_halos, *y_halos)
    peaks = lax.all_to_all(peak, "gx", 0, 0, tiled=True)
    inner, rim_first, rim_second, rim_left, rim_right = force(displacement, strength, corners, *x_halos, *y_halos)
    x_rims = swap(rim_first, rim_second, "gx")
    *x_rims, peaks = lax.optimization_barrier((*x_rims, peaks))
    peaks = jnp.broadcast_to(jnp.max(peaks, axis=0, keepdims=True), (peers_y, PTS))
    peaks = lax.all_to_all(peaks, "gy", 0, 0, tiled=True)
    above = jnp.where(even_x, x_rims[1], x_rims[0])
    below = jnp.where(even_x, x_rims[0], x_rims[1])

    def side(rim_side, c):
        return rim_side.at[:, 0].add(above[:, c]).at[:, ROWS - 1].add(below[:, c])

    west, east = side(rim_left, 0), side(rim_right, EXT_COLS - 1)
    y_rims = swap(jnp.where(even_y, east, west), jnp.where(even_y, west, east), "gy")
    return damage, finish(inner, *x_rims, *y_rims, peaks)[0]


def solution(mesh):
    spec = P(None, "gx", "gy", None)
    in_specs = (spec, spec, spec, spec, P(None, "gx", "gy"), spec)
    return jax.shard_map(local, mesh=mesh, in_specs=in_specs, out_specs=(spec, spec), check_vma=False)
```

```python
import jax
import jax.numpy as jnp
from jax import lax
from jax.experimental import pallas as pl
from jax.experimental.pallas import tpu as pltpu
from jax.sharding import PartitionSpec as P

PTS = 128
LAYERS = 5
ROWS = 4
COLS = 16
EXT_ROWS = ROWS + 2
LAST = ROWS + 1
EXT_COLS = COLS + 2
STRAIN_SCALE = 0.05
INV_RADIUS = 0.1
SPREAD_LIMIT = 128.0
SLOT_OF = {(0, 0): 0, (-1, -1): 1, (-1, 0): 2, (-1, 1): 3, (0, -1): 4, (0, 1): 5, (1, -1): 6, (1, 0): 7, (1, 1): 8}
PIECES = 32
RAW = 24
TILES = ROWS * COLS
DISP_COLS = 24
INSIDE = [(o, r) for r in range(ROWS) for o in range(ROWS) if abs(o - r) <= 1]
V_ROWS = (0, 3, 6, 9, 12, 15)
MIB = 1024 * 1024


def split3(value):
    hi = value.astype(jnp.bfloat16).astype(jnp.float32)
    rest = value - hi
    mid = rest.astype(jnp.bfloat16).astype(jnp.float32)
    return hi, mid, rest - mid


def scaled(xyz, centre):
    a = [(xyz[x] - centre[x]) * INV_RADIUS for x in range(3)]
    return a, a[0] * a[0] + a[1] * a[1] + a[2] * a[2]


def centre_of(coords):
    return [0.5 * (jnp.min(coords[x]) + jnp.max(coords[x])) for x in range(3)]


def put_other(sv, a, norm, at):
    for x in range(3):
        hi, mid, lo = split3(a[x])
        for k, v in zip(V_ROWS, (hi, hi, mid, mid, hi, lo)):
            sv[at(k + x), :] = v
    for k, v in enumerate(split3(-norm)):
        sv[at(21 + k), :] = v


def put_own(su, a, norm, xyz, at):
    for x in range(3):
        hi, mid, lo = split3(a[x])
        for k, v in zip(V_ROWS, (hi, mid, hi, mid, lo, hi)):
            su[at(k + x), :] = 2.0 * v
        su[at(RAW + x), :] = xyz[x]
    for k, v in enumerate(split3(1.0 - norm)):
        su[at(18 + k), :] = v


def constant_rows():
    row8 = lax.broadcasted_iota(jnp.int32, (8, PTS), 0)
    other = jnp.where((row8 >= 2) & (row8 <= 4), 1.0, 0.0)
    own = jnp.where(row8 >= 5, 1.0, 0.0)
    ones = jnp.where(row8 == LAYERS, 1.0, 0.0)
    return other.astype(jnp.float32), own.astype(jnp.float32), ones.astype(jnp.float32)


def rows_at(index, size, count=None):
    return pl.ds(pl.multiple_of(index * size, size), size if count is None else count)


def bell_weights(other, own):
    bell = jnp.maximum(jnp.dot(other, own, preferred_element_type=jnp.float32), 0.0)
    return (bell * bell).astype(jnp.bfloat16)


def direct_total(own, other, values):
    turned = jnp.concatenate([other] + [jnp.zeros((8, PTS), jnp.float32)] * 15, axis=0).T
    dist = jnp.zeros((PTS, PTS), jnp.float32)
    for x in range(3):
        dist = dist + (own[x : x + 1, :] - turned[:, x : x + 1]) ** 2
    bell = jnp.maximum(1.0 - dist * 0.01, 0.0)
    pair = (bell * bell).astype(jnp.bfloat16)
    return jnp.dot(values.astype(jnp.bfloat16), pair, preferred_element_type=jnp.float32)


def is_live(links, dr, dc, r, c):
    return jnp.where(links[SLOT_OF[(dr, dc)], r, c] >= 0, 1.0, 0.0).astype(jnp.float32)


def facing(first, second, axis):
    even = lax.axis_index(axis) % 2 == 0
    return (lambda i: jnp.where(even, second[i], first[i])), (lambda i: jnp.where(even, first[i], second[i]))


def split_body(strain, coords, su, vt, src, info, sv):
    f32, bf16 = jnp.float32, jnp.bfloat16
    other_const, own_const, ones = constant_rows()
    zero8 = jnp.zeros((8, PTS), f32)
    for c in range(EXT_COLS):
        edge = c in (0, EXT_COLS - 1)
        for r in range(ROWS):
            src[pl.ds((c * ROWS + r) * 8, 8), :] = zero8 if edge else ones
            if not edge:
                sv[pl.ds(((c - 1) * ROWS + r) * PIECES + 16, 8), :] = other_const
                sv[pl.ds(((c - 1) * ROWS + r) * PIECES + 24, 8), :] = zero8
    for t in range(TILES):
        su[pl.ds(t * PIECES + 16, 8), :] = own_const
        su[pl.ds(t * PIECES + 24, 8), :] = zero8
    for c in (0, EXT_COLS - 1):
        vt[pl.ds(c * PTS, PTS), :] = jnp.zeros((PTS, PTS), bf16)

    centre = centre_of(coords)
    far = jnp.zeros((COLS, PTS), f32)
    step = ROWS * PIECES
    for r in range(ROWS):
        xyz = [coords[x, r] for x in range(3)]
        a, norm = scaled(xyz, centre)
        far = jnp.maximum(far, norm)
        put_other(sv, a, norm, lambda k: pl.ds(r * PIECES + k, COLS, stride=step))
        put_own(su, a, norm, xyz, lambda k: pl.ds(r * PIECES + k, COLS, stride=step))
        for l in range(LAYERS):
            src[pl.ds((ROWS + r) * 8 + l, COLS, stride=ROWS * 8), :] = strain[l, r]
    info[...] = jnp.zeros(info.shape, f32)
    for x in range(3):
        info[x : x + 1] = jnp.full((1, PTS), centre[x], f32)
    info[3:4] = jnp.max(far, axis=0, keepdims=True)

    def turn(c, carry):
        vt[rows_at(c + 1, PTS), :] = sv[rows_at(c, step), :].T.astype(bf16)
        return carry

    lax.fori_loop(0, COLS, turn, 0, unroll=8)


def inside_body(links, su, vt, src, info, totals, block, weights):
    f32, bf16 = jnp.float32, jnp.bfloat16
    zero8 = jnp.zeros((8, PTS), f32)
    block[...] = jnp.zeros(block.shape, bf16)
    near = jnp.max(info[3:4]) <= SPREAD_LIMIT

    @pl.when(near)
    def _():
        def column(c, carry):
            for j, (o, r) in enumerate(INSIDE):
                own = su[rows_at(c * ROWS + r, PIECES), :]
                block[pl.ds(o * PIECES, PIECES), pl.ds(j * PTS, PTS)] = own.astype(bf16)
            others = vt[rows_at(c, PTS, 3 * PTS), :]
            for j in range(0, len(INSIDE), 2):
                weights[:, j * PTS : (j + 2) * PTS] = bell_weights(others, block[:, j * PTS : (j + 2) * PTS])
            sums = [zero8 for _ in range(ROWS)]
            for j in range(0, len(INSIDE), 2):
                halves = []
                for o, r in INSIDE[j : j + 2]:
                    parts = [src[rows_at((c + dc) * ROWS + o, 8), :] * is_live(links, o - r, dc - 1, r, c) for dc in range(3)]
                    halves.append(jnp.concatenate(parts, axis=1))
                values = jnp.concatenate(halves, axis=0).astype(bf16)
                out = jnp.dot(values, weights[:, j * PTS : (j + 2) * PTS], preferred_element_type=f32)
                for h in range(2):
                    r = INSIDE[j + h][1]
                    sums[r] = sums[r] + out[8 * h : 8 * h + 8, h * PTS : (h + 1) * PTS]
            for r in range(ROWS):
                totals[pl.ds(r * COLS + c, 8, stride=TILES), :] = sums[r]
            return carry

        lax.fori_loop(0, COLS, column, 0, unroll=16)

    @pl.when(jnp.logical_not(near))
    def _():
        def tile(t, carry):
            r, c = t // COLS, t % COLS
            own = su[pl.ds(pl.multiple_of((c * ROWS + r) * PIECES + RAW, 8), 8), :]
            total = zero8
            for (dr, dc), slot in SLOT_OF.items():
                within = (r + dr >= 0) & (r + dr < ROWS) & (c + dc >= 0) & (c + dc < COLS) & (links[slot, r, c] >= 0)
                o = jnp.minimum(jnp.maximum(r + dr, 0), ROWS - 1)
                oc = jnp.minimum(jnp.maximum(c + dc, 0), COLS - 1)
                other = su[pl.ds(pl.multiple_of((oc * ROWS + o) * PIECES + RAW, 8), 8), :]
                values = src[rows_at((oc + 1) * ROWS + o, 8), :] * jnp.where(within, 1.0, 0.0)
                total = total + direct_total(own, other, values)
            totals[pl.ds(t, 8, stride=TILES), :] = total
            return carry

        lax.fori_loop(0, TILES, tile, 0)


def rim_body(
    stiff, links, inside, su, info, x_first, x_second, y_first, y_second,
    damage, strength, peak,
    sv, sides, vt, vt_sides, block, block_sides, weights, src, raw, totals,
):
    before, after = facing(x_first, x_second, "gx")
    left, right = facing(y_first, y_second, "gy")
    f32, bf16 = jnp.float32, jnp.bfloat16
    gx, gy = lax.axis_index("gx"), lax.axis_index("gy")
    has_top, has_bot = gx > 0, gx < lax.axis_size("gx") - 1
    has_left, has_right = gy > 0, gy < lax.axis_size("gy") - 1
    other_const, _, ones = constant_rows()
    zero8 = jnp.zeros((8, PTS), f32)
    totals[...] = inside[...]
    for c in range(EXT_COLS):
        for h in range(2):
            sv[pl.ds(c * PTS + h * PIECES + 16, 8), :] = other_const
            sv[pl.ds(c * PTS + h * PIECES + 24, 8), :] = zero8
            src[pl.ds(((h * LAST) * EXT_COLS + c) * 8, 8), :] = ones
        sv[pl.ds(c * PTS + 64, 64), :] = jnp.zeros((64, PTS), f32)
    for r in range(ROWS):
        for h in range(2):
            sides[pl.ds((h * ROWS + r) * PIECES + 16, 8), :] = other_const
            sides[pl.ds((h * ROWS + r) * PIECES + 24, 8), :] = zero8
            src[pl.ds(((r + 1) * EXT_COLS + h * (EXT_COLS - 1)) * 8, 8), :] = ones
    block[...] = jnp.zeros(block.shape, bf16)
    block_sides[...] = jnp.zeros(block_sides.shape, bf16)

    centre = [info[x : x + 1, :] for x in range(3)]
    far = jnp.broadcast_to(info[3:4, :], (COLS, PTS))
    for h, halo, there in ((0, before, has_top), (1, after, has_bot)):
        xyz = [halo(x) for x in range(3)]
        a, norm = scaled(xyz, centre)
        far = jnp.maximum(far, jnp.where(there, norm, 0.0))
        put_other(sv, a, norm, lambda k: pl.ds(PTS + h * PIECES + k, COLS, stride=PTS))
        first = (h * LAST * EXT_COLS + 1) * 8
        for x in range(3):
            raw[pl.ds(first + x, COLS, stride=8), :] = xyz[x]
        for l in range(LAYERS):
            src[pl.ds(first + l, COLS, stride=8), :] = halo(3 + l)
    rows6 = lax.broadcasted_iota(jnp.int32, (EXT_ROWS, PTS), 0)
    there6 = ((rows6 > 0) | has_top) & ((rows6 < LAST) | has_bot)
    side = jnp.zeros((EXT_ROWS, PTS), f32)
    for h, halo, there in ((0, left, has_left), (1, right, has_right)):
        xyz = [halo(x) for x in range(3)]
        a, norm = scaled(xyz, centre)
        side = jnp.maximum(side, jnp.where(there6 & there, norm, 0.0))
        mid = [v[1:LAST] for v in a]
        put_other(sides, mid, norm[1:LAST], lambda k: pl.ds(h * ROWS * PIECES + k, ROWS, stride=PIECES))
        col = h * (EXT_COLS - 1)
        for e in range(2):
            one = slice(e * LAST, e * LAST + 1)
            put_other(sv, [v[one] for v in a], norm[one], lambda k: pl.ds(col * PTS + e * PIECES + k, 1))
        for x in range(3):
            raw[pl.ds(col * 8 + x, EXT_ROWS, stride=EXT_COLS * 8), :] = xyz[x]
        for l in range(LAYERS):
            src[pl.ds(col * 8 + l, EXT_ROWS, stride=EXT_COLS * 8), :] = halo(3 + l)
    near = jnp.maximum(jnp.max(far), jnp.max(side)) <= SPREAD_LIMIT

    def add(r, c, value):
        at = pl.ds(r * COLS + c, 8, stride=TILES)
        totals[at, :] = totals[at, :] + value

    @pl.when(near)
    def _():
        def turn(c, carry):
            vt[rows_at(c, PTS), :] = sv[rows_at(c, PTS), :].T.astype(bf16)
            return carry

        lax.fori_loop(0, EXT_COLS, turn, 0, unroll=18)
        vt_sides[...] = sides[...].T.astype(bf16)
        for h in range(2):
            for j, (o, r) in enumerate(INSIDE):
                own = su[pl.ds((h * (COLS - 1) * ROWS + r) * PIECES, PIECES), :].astype(bf16)
                block_sides[pl.ds((h * ROWS + o) * PIECES, PIECES), pl.ds((h * len(INSIDE) + j) * PTS, PTS)] = own
        for j in range(0, 2 * len(INSIDE), 2):
            weights[pl.ds(3 * PTS * COLS + (j // 2) * PTS, PTS), :] = bell_weights(
                vt_sides[...], block_sides[:, j * PTS : (j + 2) * PTS]
            )

        def weigh(c, carry):
            for h in range(2):
                own = su[rows_at(c * ROWS + h * (ROWS - 1), PIECES), :].astype(bf16)
                block[rows_at(2 * c + h, PIECES), pl.ds(h * PTS, PTS)] = own
            here = block[rows_at(c, 2 * PIECES), :]
            own = jnp.concatenate([here, jnp.zeros((64, 2 * PTS), bf16)], axis=0)
            weights[rows_at(c, 3 * PTS), :] = bell_weights(vt[rows_at(c, PTS, 3 * PTS), :], own)
            return carry

        lax.fori_loop(0, COLS, weigh, 0, unroll=16)

        def total(c, carry):
            halves = []
            for h in range(2):
                parts = [
                    src[rows_at(h * LAST * EXT_COLS + c + dc, 8), :] * is_live(links, 2 * h - 1, dc - 1, h * (ROWS - 1), c)
                    for dc in range(3)
                ]
                halves.append(jnp.concatenate(parts, axis=1))
            values = jnp.concatenate(halves, axis=0).astype(bf16)
            out = jnp.dot(values, weights[rows_at(c, 3 * PTS), :], preferred_element_type=f32)
            for h in range(2):
                add(h * (ROWS - 1), c, out[8 * h : 8 * h + 8, h * PTS : (h + 1) * PTS])
            return carry

        lax.fori_loop(0, COLS, total, 0, unroll=16)
        sums = [[zero8 for _ in range(ROWS)] for _ in range(2)]
        for j in range(0, 2 * len(INSIDE), 2):
            halves, owners = [], []
            for i in (j, j + 1):
                h, (o, r) = i // len(INSIDE), INSIDE[i % len(INSIDE)]
                held = src[pl.ds(((o + 1) * EXT_COLS + h * (EXT_COLS - 1)) * 8, 8), :]
                halves.append(held * is_live(links, o - r, 2 * h - 1, r, h * (COLS - 1)))
                owners.append((h, r))
            values = jnp.concatenate(halves, axis=0).astype(bf16)
            pair = weights[pl.ds(3 * PTS * COLS + (j // 2) * PTS, PTS), :]
            out = jnp.dot(values, pair, preferred_element_type=f32)
            for i, (h, r) in enumerate(owners):
                sums[h][r] = sums[h][r] + out[8 * i : 8 * i + 8, i * PTS : (i + 1) * PTS]
        for h in range(2):
            for r in range(ROWS):
                add(r, h * (COLS - 1), sums[h][r])

    @pl.when(jnp.logical_not(near))
    def _():
        def tile(t, carry):
            r, c = t // COLS, t % COLS
            own = su[pl.ds(pl.multiple_of((c * ROWS + r) * PIECES + RAW, 8), 8), :]
            for (dr, dc), slot in SLOT_OF.items():
                o, oc = r + dr, c + dc
                within = (o >= 0) & (o < ROWS) & (oc >= 0) & (oc < COLS)

                @pl.when(jnp.logical_not(within) & (links[slot, r, c] >= 0))
                def _():
                    at = rows_at((o + 1) * EXT_COLS + oc + 1, 8)
                    add(r, c, direct_total(own, raw[at, :], src[at, :]))

            return carry

        lax.fori_loop(0, TILES, tile, 0)

    for r in range(ROWS):
        weight_sum = totals[pl.ds(LAYERS * TILES + r * COLS, COLS), :]
        mean = jnp.zeros((COLS, PTS), f32)
        for l in range(LAYERS):
            averaged = totals[pl.ds(l * TILES + r * COLS, COLS), :] / weight_sum
            value = averaged / (averaged + STRAIN_SCALE)
            damage[l, r] = value
            mean = mean + value
        power = (1.0 - mean / LAYERS) * stiff[0, r]
        strength[r] = power
        top = jnp.maximum(top, power) if r else power
    peak[...] = jnp.full(peak.shape, jnp.max(top), f32)


def force_body(
    disp, strength, corners, x_first, x_second, y_first, y_second,
    inner, rim_first, rim_second, rim_left, rim_right,
    edisp, amounts, forces,
):
    f32, bf16 = jnp.float32, jnp.bfloat16
    before, after = facing(x_first, x_second, "gx")
    left, right = facing(y_first, y_second, "gy")
    even = lax.axis_index("gx") % 2 == 0
    forces[...] = jnp.zeros(forces.shape, f32)
    for x in range(3):
        for r in range(EXT_ROWS):
            row = before(8 + x) if r == 0 else after(8 + x) if r == LAST else disp[x, r - 1]
            edisp[pl.ds((x * EXT_ROWS + r) * DISP_COLS + 1, COLS), :] = row
        edisp[pl.ds(x * EXT_ROWS * DISP_COLS, EXT_ROWS, stride=DISP_COLS), :] = left(8 + x)
        edisp[pl.ds(x * EXT_ROWS * DISP_COLS + COLS + 1, EXT_ROWS, stride=DISP_COLS), :] = right(8 + x)

    def gather(r, carry):
        for g in range(COLS // 8):
            power = strength[r, 8 * g : 8 * g + 8, :]
            codes = [corners[k, r, 8 * g : 8 * g + 8, :] for k in range(4)]
            offset = [code >> 7 for code in codes]
            slot = [code & (PTS - 1) for code in codes]
            at = [
                pl.ds(pl.multiple_of(((r * COLS + 8 * g) * 4 + k) * 8, 8) + i, 8, stride=32)
                for k in range(4) for i in range(8)
            ]
            for k in range(4):
                amounts[at[8 * k + 3], :] = offset[k].astype(f32)
                amounts[at[8 * k + 7], :] = slot[k].astype(f32)
            for x in range(3):
                picked = []
                base = (x * EXT_ROWS + r) * DISP_COLS + 8 * g
                table = [edisp[pl.ds(base + (o // 3) * DISP_COLS + o % 3, 8), :] for o in range(9)]
                for k in range(4):
                    found = jnp.take_along_axis(table[0], slot[k], axis=1)
                    for o in range(1, 9):
                        found = jnp.where(offset[k] == o, jnp.take_along_axis(table[o], slot[k], axis=1), found)
                    picked.append(found)
                springs = [power * (picked[(k + 1) % 4] - picked[k]) for k in range(4)]
                for k in range(4):
                    amount = springs[k] - springs[(k + 3) % 4]
                    hi = amount.astype(bf16).astype(f32)
                    amounts[at[8 * k + x], :] = hi
                    amounts[at[8 * k + 4 + x], :] = amount - hi
        return carry

    lax.fori_loop(0, ROWS, gather, 0, unroll=4)

    nodes = lax.broadcasted_iota(jnp.int32, (PTS, PTS), 0).astype(f32)

    def scatter(t, carry):
        r, c = t // COLS, t % COLS
        picks, rows = [], []
        for k in range(4):
            own = amounts[pl.ds(pl.multiple_of((t * 4 + k) * 8, 8), 8), :]
            offset, slot = own[3:4, :], own[7:8, :]
            rows.append(jnp.concatenate([jnp.where(offset == float(o), own, 0.0) for o in range(10)], axis=0))
            picks.append(jnp.where(slot == nodes, 1.0, 0.0).astype(bf16))
        left_side = jnp.concatenate(rows, axis=1).astype(bf16)
        right_side = jnp.concatenate(picks, axis=1)
        out = lax.dot_general(left_side, right_side, (((1,), (1,)), ((), ())), preferred_element_type=f32)
        for o in range(9):
            at = pl.ds(pl.multiple_of(((r + o // 3) * EXT_COLS + c + o % 3) * 8, 8), 8)
            forces[at, :] = forces[at, :] + out[8 * o : 8 * o + 8]
        return carry

    lax.fori_loop(0, ROWS * COLS, scatter, 0, unroll=32)

    def node_sum(x, first, count, stride):
        return (
            forces[pl.ds(first * 8 + x, count, stride=8 * stride), :]
            + forces[pl.ds(first * 8 + 4 + x, count, stride=8 * stride), :]
        )

    for x in range(3):
        for r in range(ROWS):
            inner[x, r] = node_sum(x, (r + 1) * EXT_COLS + 1, COLS, 1)
        top = node_sum(x, 0, EXT_COLS, 1)
        bottom = node_sum(x, LAST * EXT_COLS, EXT_COLS, 1)
        rim_first[x] = jnp.where(even, bottom, top)
        rim_second[x] = jnp.where(even, top, bottom)
        rim_left[x] = node_sum(x, EXT_COLS, ROWS, EXT_COLS)
        rim_right[x] = node_sum(x, 2 * EXT_COLS - 1, ROWS, EXT_COLS)


def finish_body(inner, x_first, x_second, y_first, y_second, peaks, out):
    before, after = facing(x_first, x_second, "gx")
    left, right = facing(y_first, y_second, "gy")
    top = jnp.max(peaks[...])
    cols = lax.broadcasted_iota(jnp.int32, (COLS, PTS), 0)
    for x in range(3):
        west, east = left(x), right(x)
        for r in range(ROWS):
            value = inner[x, r]
            if r == 0:
                value = value + before(x)[1 : COLS + 1]
            if r == ROWS - 1:
                value = value + after(x)[1 : COLS + 1]
            value = value + jnp.where(cols == 0, west[r : r + 1], 0.0) + jnp.where(cols == COLS - 1, east[r : r + 1], 0.0)
            out[x, r] = value / top


def kernels(peers):
    f32, bf16 = jnp.float32, jnp.bfloat16
    vmem = pl.BlockSpec(memory_space=pltpu.VMEM)
    smem = pl.BlockSpec(memory_space=pltpu.SMEM)

    def call(body, name, ins, outs, scratch, flops):
        return pl.pallas_call(
            body,
            out_shape=tuple(jax.ShapeDtypeStruct(*o) for o in outs),
            in_specs=[smem if i == "links" else vmem for i in ins],
            out_specs=(vmem,) * len(outs),
            scratch_shapes=[pltpu.VMEM(*v) for v in scratch],
            compiler_params=pltpu.CompilerParams(vmem_limit_bytes=24 * MIB),
            cost_estimate=pl.CostEstimate(flops=flops, bytes_accessed=MIB, transcendentals=0),
            name=name,
        )

    split = call(
        split_body,
        "split_block",
        ("strain", "coords"),
        [
            ((TILES * PIECES, PTS), f32),
            ((EXT_COLS * PTS, PTS), bf16),
            ((EXT_COLS * ROWS * 8, PTS), f32),
            ((8, PTS), f32),
        ],
        [((TILES * PIECES, PTS), f32)],
        3 * 10**9,
    )
    inside = call(
        inside_body,
        "inside_links",
        ("links", "su", "vt", "src", "info"),
        [((8 * TILES, PTS), f32)],
        [
            ((PTS, len(INSIDE) * PTS), bf16),
            ((3 * PTS, len(INSIDE) * PTS), bf16),
        ],
        6 * 10**9,
    )
    rim = call(
        rim_body,
        "rim_links",
        ("stiff", "links", "inside", "su", "info", "x_first", "x_second", "y_first", "y_second"),
        [((LAYERS, ROWS, COLS, PTS), f32), ((ROWS, COLS, PTS), f32), ((peers, PTS), f32)],
        [
            ((EXT_COLS * PTS, PTS), f32),
            ((2 * PTS, PTS), f32),
            ((EXT_COLS * PTS, PTS), bf16),
            ((PTS, 2 * PTS), bf16),
            ((COLS * 2 * PIECES, 2 * PTS), bf16),
            ((2 * PTS, 2 * len(INSIDE) * PTS), bf16),
            ((3 * PTS * COLS + len(INSIDE) * PTS, 2 * PTS), bf16),
            ((EXT_ROWS * EXT_COLS * 8, PTS), f32),
            ((EXT_ROWS * EXT_COLS * 8, PTS), f32),
            ((8 * TILES, PTS), f32),
        ],
        4 * 10**9,
    )
    force = call(
        force_body,
        "node_forces",
        ("disp", "strength", "corners", "x_first", "x_second", "y_first", "y_second"),
        [
            ((3, ROWS, COLS, PTS), f32),
            ((3, EXT_COLS, PTS), f32),
            ((3, EXT_COLS, PTS), f32),
            ((3, ROWS, PTS), f32),
            ((3, ROWS, PTS), f32),
        ],
        [
            ((3 * EXT_ROWS * DISP_COLS, PTS), f32),
            ((TILES * 32, PTS), f32),
            ((EXT_ROWS * EXT_COLS * 8, PTS), f32),
        ],
        8 * 10**9,
    )
    finish = call(
        finish_body,
        "finish",
        ("inner", "x_first", "x_second", "y_first", "y_second", "peaks"),
        [((3, ROWS, COLS, PTS), f32)],
        [],
        10**6,
    )
    return split, inside, rim, force, finish


def swap(first, second, axis):
    peers = lax.axis_size(axis)
    with_first = [(i, i ^ 1) for i in range(peers)]
    with_second = [(i, ((i - 1) ^ 1) + 1) for i in range(1, peers - 1)]
    return lax.ppermute(first, axis, with_first), lax.ppermute(second, axis, with_second)


def local(strain, coords, displacement, stiffness, neighbours, corners):
    peers_x, peers_y = lax.axis_size("gx"), lax.axis_size("gy")
    even_x, even_y = lax.axis_index("gx") % 2 == 0, lax.axis_index("gy") % 2 == 0
    own = (coords, strain, displacement)

    def take(value, index, dim):
        return lax.dynamic_index_in_dim(value, index, dim, keepdims=False)

    def row(r):
        return jnp.concatenate([take(v, r, 1) for v in own], axis=0)

    split, inside, rim, force, finish = kernels(peers_x)
    x_halos = swap(row(jnp.where(even_x, ROWS - 1, 0)), row(jnp.where(even_x, 0, ROWS - 1)), "gx")
    pieces = split(strain, coords)
    *x_halos, pieces = lax.optimization_barrier((*x_halos, pieces))
    above = jnp.where(even_x, x_halos[1], x_halos[0])
    below = jnp.where(even_x, x_halos[0], x_halos[1])

    def column(c):
        mid = jnp.concatenate([take(v, c, 2) for v in own], axis=0)
        return jnp.concatenate([take(above, c, 1)[:, None], mid, take(below, c, 1)[:, None]], axis=1)

    y_halos = swap(column(jnp.where(even_y, COLS - 1, 0)), column(jnp.where(even_y, 0, COLS - 1)), "gy")
    own_pieces, _, _, info = pieces
    totals = inside(neighbours, *pieces)[0]
    damage, strength, peak = rim(stiffness, neighbours, totals, own_pieces, info, *x_halos, *y_halos)
    peaks = lax.all_to_all(peak, "gx", 0, 0, tiled=True)
    inner, rim_first, rim_second, rim_left, rim_right = force(displacement, strength, corners, *x_halos, *y_halos)
    rim_first, rim_second, peaks = lax.optimization_barrier((rim_first, rim_second, peaks))
    x_rims = swap(rim_first, rim_second, "gx")
    peaks = jnp.broadcast_to(jnp.max(peaks, axis=0, keepdims=True), (peers_y, PTS))
    peaks = lax.all_to_all(peaks, "gy", 0, 0, tiled=True)
    above = jnp.where(even_x, x_rims[1], x_rims[0])
    below = jnp.where(even_x, x_rims[0], x_rims[1])

    def side(rim_side, c):
        return rim_side.at[:, 0].add(above[:, c]).at[:, ROWS - 1].add(below[:, c])

    west, east = side(rim_left, 0), side(rim_right, EXT_COLS - 1)
    y_rims = swap(jnp.where(even_y, east, west), jnp.where(even_y, west, east), "gy")
    return damage, finish(inner, *x_rims, *y_rims, peaks)[0]


def solution(mesh):
    spec = P(None, "gx", "gy", None)
    in_specs = (spec, spec, spec, spec, P(None, "gx", "gy"), spec)
    return jax.shard_map(local, mesh=mesh, in_specs=in_specs, out_specs=(spec, spec), check_vma=False)
```

```python
import jax
import jax.numpy as jnp
from jax import lax
from jax.experimental import pallas as pl
from jax.experimental.pallas import tpu as pltpu
from jax.sharding import PartitionSpec as P

PTS = 128
LAYERS = 5
ROWS = 4
COLS = 16
EXT_ROWS = ROWS + 2
LAST = ROWS + 1
EXT_COLS = COLS + 2
STRAIN_SCALE = 0.05
INV_RADIUS = 0.1
SPREAD_LIMIT = 128.0
SLOT_OF = {(0, 0): 0, (-1, -1): 1, (-1, 0): 2, (-1, 1): 3, (0, -1): 4, (0, 1): 5, (1, -1): 6, (1, 0): 7, (1, 1): 8}
PIECES = 32
RAW = 24
TILES = ROWS * COLS
DISP_COLS = 24
INSIDE = [(o, r) for r in range(ROWS) for o in range(ROWS) if abs(o - r) <= 1]
V_ROWS = (0, 3, 6, 9, 12, 15)
MIB = 1024 * 1024


def split3(value):
    hi = value.astype(jnp.bfloat16).astype(jnp.float32)
    rest = value - hi
    mid = rest.astype(jnp.bfloat16).astype(jnp.float32)
    return hi, mid, rest - mid


def scaled(xyz, centre):
    a = [(xyz[x] - centre[x]) * INV_RADIUS for x in range(3)]
    return a, a[0] * a[0] + a[1] * a[1] + a[2] * a[2]


def centre_of(coords):
    return [0.5 * (jnp.min(coords[x]) + jnp.max(coords[x])) for x in range(3)]


def put_other(sv, a, norm, at):
    for x in range(3):
        hi, mid, lo = split3(a[x])
        for k, v in zip(V_ROWS, (hi, hi, mid, mid, hi, lo)):
            sv[at(k + x), :] = v
    for k, v in enumerate(split3(-norm)):
        sv[at(21 + k), :] = v


def put_own(su, a, norm, xyz, at):
    for x in range(3):
        hi, mid, lo = split3(a[x])
        for k, v in zip(V_ROWS, (hi, mid, hi, mid, lo, hi)):
            su[at(k + x), :] = 2.0 * v
        su[at(RAW + x), :] = xyz[x]
    for k, v in enumerate(split3(1.0 - norm)):
        su[at(18 + k), :] = v


def constant_rows():
    row8 = lax.broadcasted_iota(jnp.int32, (8, PTS), 0)
    other = jnp.where((row8 >= 2) & (row8 <= 4), 1.0, 0.0)
    own = jnp.where(row8 >= 5, 1.0, 0.0)
    ones = jnp.where(row8 == LAYERS, 1.0, 0.0)
    return other.astype(jnp.float32), own.astype(jnp.float32), ones.astype(jnp.float32)


def rows_at(index, size, count=None):
    return pl.ds(pl.multiple_of(index * size, size), size if count is None else count)


def bell_weights(other, own):
    bell = jnp.maximum(jnp.dot(other, own, preferred_element_type=jnp.float32), 0.0)
    return (bell * bell).astype(jnp.bfloat16)


def direct_total(own, other, values):
    turned = jnp.concatenate([other] + [jnp.zeros((8, PTS), jnp.float32)] * 15, axis=0).T
    dist = jnp.zeros((PTS, PTS), jnp.float32)
    for x in range(3):
        dist = dist + (own[x : x + 1, :] - turned[:, x : x + 1]) ** 2
    bell = jnp.maximum(1.0 - dist * 0.01, 0.0)
    pair = (bell * bell).astype(jnp.bfloat16)
    return jnp.dot(values.astype(jnp.bfloat16), pair, preferred_element_type=jnp.float32)


def is_live(links, dr, dc, r, c):
    return jnp.where(links[SLOT_OF[(dr, dc)], r, c] >= 0, 1.0, 0.0).astype(jnp.float32)


def facing(first, second, axis):
    even = lax.axis_index(axis) % 2 == 0
    return (lambda i: jnp.where(even, second[i], first[i])), (lambda i: jnp.where(even, first[i], second[i]))


def split_body(strain, coords, su, vt, src, info, sv):
    f32, bf16 = jnp.float32, jnp.bfloat16
    other_const, own_const, ones = constant_rows()
    zero8 = jnp.zeros((8, PTS), f32)
    for c in range(EXT_COLS):
        edge = c in (0, EXT_COLS - 1)
        for r in range(ROWS):
            src[pl.ds((c * ROWS + r) * 8, 8), :] = zero8 if edge else ones
            if not edge:
                sv[pl.ds(((c - 1) * ROWS + r) * PIECES + 16, 8), :] = other_const
                sv[pl.ds(((c - 1) * ROWS + r) * PIECES + 24, 8), :] = zero8
    for t in range(TILES):
        su[pl.ds(t * PIECES + 16, 8), :] = own_const
        su[pl.ds(t * PIECES + 24, 8), :] = zero8
    for c in (0, EXT_COLS - 1):
        vt[pl.ds(c * PTS, PTS), :] = jnp.zeros((PTS, PTS), bf16)

    centre = centre_of(coords)
    far = jnp.zeros((COLS, PTS), f32)
    step = ROWS * PIECES
    for r in range(ROWS):
        xyz = [coords[x, r] for x in range(3)]
        a, norm = scaled(xyz, centre)
        far = jnp.maximum(far, norm)
        put_other(sv, a, norm, lambda k: pl.ds(r * PIECES + k, COLS, stride=step))
        put_own(su, a, norm, xyz, lambda k: pl.ds(r * PIECES + k, COLS, stride=step))
        for l in range(LAYERS):
            src[pl.ds((ROWS + r) * 8 + l, COLS, stride=ROWS * 8), :] = strain[l, r]
    info[...] = jnp.zeros(info.shape, f32)
    for x in range(3):
        info[x : x + 1] = jnp.full((1, PTS), centre[x], f32)
    info[3:4] = jnp.max(far, axis=0, keepdims=True)

    def turn(c, carry):
        vt[rows_at(c + 1, PTS), :] = sv[rows_at(c, step), :].T.astype(bf16)
        return carry

    lax.fori_loop(0, COLS, turn, 0, unroll=8)


def inside_body(links, su, vt, src, info, totals, block, weights):
    f32, bf16 = jnp.float32, jnp.bfloat16
    zero8 = jnp.zeros((8, PTS), f32)
    block[...] = jnp.zeros(block.shape, bf16)
    near = jnp.max(info[3:4]) <= SPREAD_LIMIT

    @pl.when(near)
    def _():
        def column(c, carry):
            for j, (o, r) in enumerate(INSIDE):
                own = su[rows_at(c * ROWS + r, PIECES), :]
                block[pl.ds(o * PIECES, PIECES), pl.ds(j * PTS, PTS)] = own.astype(bf16)
            others = vt[rows_at(c, PTS, 3 * PTS), :]
            for j in range(0, len(INSIDE), 2):
                weights[:, j * PTS : (j + 2) * PTS] = bell_weights(others, block[:, j * PTS : (j + 2) * PTS])
            sums = [zero8 for _ in range(ROWS)]
            for j in range(0, len(INSIDE), 2):
                halves = []
                for o, r in INSIDE[j : j + 2]:
                    parts = [src[rows_at((c + dc) * ROWS + o, 8), :] * is_live(links, o - r, dc - 1, r, c) for dc in range(3)]
                    halves.append(jnp.concatenate(parts, axis=1))
                values = jnp.concatenate(halves, axis=0).astype(bf16)
                out = jnp.dot(values, weights[:, j * PTS : (j + 2) * PTS], preferred_element_type=f32)
                for h in range(2):
                    r = INSIDE[j + h][1]
                    sums[r] = sums[r] + out[8 * h : 8 * h + 8, h * PTS : (h + 1) * PTS]
            for r in range(ROWS):
                totals[pl.ds(r * COLS + c, 8, stride=TILES), :] = sums[r]
            return carry

        lax.fori_loop(0, COLS, column, 0, unroll=16)

    @pl.when(jnp.logical_not(near))
    def _():
        def tile(t, carry):
            r, c = t // COLS, t % COLS
            own = su[pl.ds(pl.multiple_of((c * ROWS + r) * PIECES + RAW, 8), 8), :]
            total = zero8
            for (dr, dc), slot in SLOT_OF.items():
                within = (r + dr >= 0) & (r + dr < ROWS) & (c + dc >= 0) & (c + dc < COLS) & (links[slot, r, c] >= 0)
                o = jnp.minimum(jnp.maximum(r + dr, 0), ROWS - 1)
                oc = jnp.minimum(jnp.maximum(c + dc, 0), COLS - 1)
                other = su[pl.ds(pl.multiple_of((oc * ROWS + o) * PIECES + RAW, 8), 8), :]
                values = src[rows_at((oc + 1) * ROWS + o, 8), :] * jnp.where(within, 1.0, 0.0)
                total = total + direct_total(own, other, values)
            totals[pl.ds(t, 8, stride=TILES), :] = total
            return carry

        lax.fori_loop(0, TILES, tile, 0)


def rim_body(
    stiff, links, inside, su, info, x_first, x_second, y_first, y_second,
    damage, strength, peak,
    sv, sides, vt, vt_sides, block, block_sides, weights, src, raw, totals,
):
    before, after = facing(x_first, x_second, "gx")
    left, right = facing(y_first, y_second, "gy")
    f32, bf16 = jnp.float32, jnp.bfloat16
    gx, gy = lax.axis_index("gx"), lax.axis_index("gy")
    has_top, has_bot = gx > 0, gx < lax.axis_size("gx") - 1
    has_left, has_right = gy > 0, gy < lax.axis_size("gy") - 1
    other_const, _, ones = constant_rows()
    zero8 = jnp.zeros((8, PTS), f32)
    totals[...] = inside[...]
    for c in range(EXT_COLS):
        for h in range(2):
            sv[pl.ds(c * PTS + h * PIECES + 16, 8), :] = other_const
            sv[pl.ds(c * PTS + h * PIECES + 24, 8), :] = zero8
            src[pl.ds(((h * LAST) * EXT_COLS + c) * 8, 8), :] = ones
        sv[pl.ds(c * PTS + 64, 64), :] = jnp.zeros((64, PTS), f32)
    for r in range(ROWS):
        for h in range(2):
            sides[pl.ds((h * ROWS + r) * PIECES + 16, 8), :] = other_const
            sides[pl.ds((h * ROWS + r) * PIECES + 24, 8), :] = zero8
            src[pl.ds(((r + 1) * EXT_COLS + h * (EXT_COLS - 1)) * 8, 8), :] = ones
    block[...] = jnp.zeros(block.shape, bf16)
    block_sides[...] = jnp.zeros(block_sides.shape, bf16)

    centre = [info[x : x + 1, :] for x in range(3)]
    far = jnp.broadcast_to(info[3:4, :], (COLS, PTS))
    for h, halo, there in ((0, before, has_top), (1, after, has_bot)):
        xyz = [halo(x) for x in range(3)]
        a, norm = scaled(xyz, centre)
        far = jnp.maximum(far, jnp.where(there, norm, 0.0))
        put_other(sv, a, norm, lambda k: pl.ds(PTS + h * PIECES + k, COLS, stride=PTS))
        first = (h * LAST * EXT_COLS + 1) * 8
        for x in range(3):
            raw[pl.ds(first + x, COLS, stride=8), :] = xyz[x]
        for l in range(LAYERS):
            src[pl.ds(first + l, COLS, stride=8), :] = halo(3 + l)
    rows6 = lax.broadcasted_iota(jnp.int32, (EXT_ROWS, PTS), 0)
    there6 = ((rows6 > 0) | has_top) & ((rows6 < LAST) | has_bot)
    side = jnp.zeros((EXT_ROWS, PTS), f32)
    for h, halo, there in ((0, left, has_left), (1, right, has_right)):
        xyz = [halo(x) for x in range(3)]
        a, norm = scaled(xyz, centre)
        side = jnp.maximum(side, jnp.where(there6 & there, norm, 0.0))
        mid = [v[1:LAST] for v in a]
        put_other(sides, mid, norm[1:LAST], lambda k: pl.ds(h * ROWS * PIECES + k, ROWS, stride=PIECES))
        col = h * (EXT_COLS - 1)
        for e in range(2):
            one = slice(e * LAST, e * LAST + 1)
            put_other(sv, [v[one] for v in a], norm[one], lambda k: pl.ds(col * PTS + e * PIECES + k, 1))
        for x in range(3):
            raw[pl.ds(col * 8 + x, EXT_ROWS, stride=EXT_COLS * 8), :] = xyz[x]
        for l in range(LAYERS):
            src[pl.ds(col * 8 + l, EXT_ROWS, stride=EXT_COLS * 8), :] = halo(3 + l)
    near = jnp.maximum(jnp.max(far), jnp.max(side)) <= SPREAD_LIMIT

    def add(r, c, value):
        at = pl.ds(r * COLS + c, 8, stride=TILES)
        totals[at, :] = totals[at, :] + value

    @pl.when(near)
    def _():
        def turn(c, carry):
            vt[rows_at(c, PTS), :] = sv[rows_at(c, PTS), :].T.astype(bf16)
            return carry

        lax.fori_loop(0, EXT_COLS, turn, 0, unroll=18)
        vt_sides[...] = sides[...].T.astype(bf16)
        for h in range(2):
            for j, (o, r) in enumerate(INSIDE):
                own = su[pl.ds((h * (COLS - 1) * ROWS + r) * PIECES, PIECES), :].astype(bf16)
                block_sides[pl.ds((h * ROWS + o) * PIECES, PIECES), pl.ds((h * len(INSIDE) + j) * PTS, PTS)] = own
        for j in range(0, 2 * len(INSIDE), 2):
            weights[pl.ds(3 * PTS * COLS + (j // 2) * PTS, PTS), :] = bell_weights(
                vt_sides[...], block_sides[:, j * PTS : (j + 2) * PTS]
            )

        def weigh(c, carry):
            for h in range(2):
                own = su[rows_at(c * ROWS + h * (ROWS - 1), PIECES), :].astype(bf16)
                block[rows_at(2 * c + h, PIECES), pl.ds(h * PTS, PTS)] = own
            here = block[rows_at(c, 2 * PIECES), :]
            own = jnp.concatenate([here, jnp.zeros((64, 2 * PTS), bf16)], axis=0)
            weights[rows_at(c, 3 * PTS), :] = bell_weights(vt[rows_at(c, PTS, 3 * PTS), :], own)
            return carry

        lax.fori_loop(0, COLS, weigh, 0, unroll=16)

        def total(c, carry):
            halves = []
            for h in range(2):
                parts = [
                    src[rows_at(h * LAST * EXT_COLS + c + dc, 8), :] * is_live(links, 2 * h - 1, dc - 1, h * (ROWS - 1), c)
                    for dc in range(3)
                ]
                halves.append(jnp.concatenate(parts, axis=1))
            values = jnp.concatenate(halves, axis=0).astype(bf16)
            out = jnp.dot(values, weights[rows_at(c, 3 * PTS), :], preferred_element_type=f32)
            for h in range(2):
                add(h * (ROWS - 1), c, out[8 * h : 8 * h + 8, h * PTS : (h + 1) * PTS])
            return carry

        lax.fori_loop(0, COLS, total, 0, unroll=16)
        sums = [[zero8 for _ in range(ROWS)] for _ in range(2)]
        for j in range(0, 2 * len(INSIDE), 2):
            halves, owners = [], []
            for i in (j, j + 1):
                h, (o, r) = i // len(INSIDE), INSIDE[i % len(INSIDE)]
                held = src[pl.ds(((o + 1) * EXT_COLS + h * (EXT_COLS - 1)) * 8, 8), :]
                halves.append(held * is_live(links, o - r, 2 * h - 1, r, h * (COLS - 1)))
                owners.append((h, r))
            values = jnp.concatenate(halves, axis=0).astype(bf16)
            pair = weights[pl.ds(3 * PTS * COLS + (j // 2) * PTS, PTS), :]
            out = jnp.dot(values, pair, preferred_element_type=f32)
            for i, (h, r) in enumerate(owners):
                sums[h][r] = sums[h][r] + out[8 * i : 8 * i + 8, i * PTS : (i + 1) * PTS]
        for h in range(2):
            for r in range(ROWS):
                add(r, h * (COLS - 1), sums[h][r])

    @pl.when(jnp.logical_not(near))
    def _():
        def tile(t, carry):
            r, c = t // COLS, t % COLS
            own = su[pl.ds(pl.multiple_of((c * ROWS + r) * PIECES + RAW, 8), 8), :]
            for (dr, dc), slot in SLOT_OF.items():
                o, oc = r + dr, c + dc
                within = (o >= 0) & (o < ROWS) & (oc >= 0) & (oc < COLS)

                @pl.when(jnp.logical_not(within) & (links[slot, r, c] >= 0))
                def _():
                    at = rows_at((o + 1) * EXT_COLS + oc + 1, 8)
                    add(r, c, direct_total(own, raw[at, :], src[at, :]))

            return carry

        lax.fori_loop(0, TILES, tile, 0)

    for r in range(ROWS):
        weight_sum = totals[pl.ds(LAYERS * TILES + r * COLS, COLS), :]
        mean = jnp.zeros((COLS, PTS), f32)
        for l in range(LAYERS):
            averaged = totals[pl.ds(l * TILES + r * COLS, COLS), :] / weight_sum
            value = averaged / (averaged + STRAIN_SCALE)
            damage[l, r] = value
            mean = mean + value
        power = (1.0 - mean / LAYERS) * stiff[0, r]
        strength[r] = power
        top = jnp.maximum(top, power) if r else power
    peak[...] = jnp.full(peak.shape, jnp.max(top), f32)


def force_body(
    disp, strength, corners, x_first, x_second, y_first, y_second,
    inner, rim_first, rim_second, rim_left, rim_right,
    edisp, amounts, forces,
):
    f32, bf16 = jnp.float32, jnp.bfloat16
    before, after = facing(x_first, x_second, "gx")
    left, right = facing(y_first, y_second, "gy")
    even = lax.axis_index("gx") % 2 == 0
    forces[...] = jnp.zeros(forces.shape, f32)
    for x in range(3):
        for r in range(EXT_ROWS):
            row = before(8 + x) if r == 0 else after(8 + x) if r == LAST else disp[x, r - 1]
            edisp[pl.ds((x * EXT_ROWS + r) * DISP_COLS + 1, COLS), :] = row
        edisp[pl.ds(x * EXT_ROWS * DISP_COLS, EXT_ROWS, stride=DISP_COLS), :] = left(8 + x)
        edisp[pl.ds(x * EXT_ROWS * DISP_COLS + COLS + 1, EXT_ROWS, stride=DISP_COLS), :] = right(8 + x)

    def gather(r, carry):
        for g in range(COLS // 8):
            power = strength[r, 8 * g : 8 * g + 8, :]
            codes = [corners[k, r, 8 * g : 8 * g + 8, :] for k in range(4)]
            offset = [code >> 7 for code in codes]
            slot = [code & (PTS - 1) for code in codes]
            at = [
                pl.ds(pl.multiple_of(((r * COLS + 8 * g) * 4 + k) * 8, 8) + i, 8, stride=32)
                for k in range(4) for i in range(8)
            ]
            for k in range(4):
                amounts[at[8 * k + 3], :] = offset[k].astype(f32)
                amounts[at[8 * k + 7], :] = slot[k].astype(f32)
            for x in range(3):
                picked = []
                base = (x * EXT_ROWS + r) * DISP_COLS + 8 * g
                table = [edisp[pl.ds(base + (o // 3) * DISP_COLS + o % 3, 8), :] for o in range(9)]
                for k in range(4):
                    found = jnp.take_along_axis(table[0], slot[k], axis=1)
                    for o in range(1, 9):
                        found = jnp.where(offset[k] == o, jnp.take_along_axis(table[o], slot[k], axis=1), found)
                    picked.append(found)
                springs = [power * (picked[(k + 1) % 4] - picked[k]) for k in range(4)]
                for k in range(4):
                    amount = springs[k] - springs[(k + 3) % 4]
                    hi = amount.astype(bf16).astype(f32)
                    amounts[at[8 * k + x], :] = hi
                    amounts[at[8 * k + 4 + x], :] = amount - hi
        return carry

    lax.fori_loop(0, ROWS, gather, 0, unroll=4)

    nodes = lax.broadcasted_iota(jnp.int32, (PTS, PTS), 0).astype(f32)

    def scatter(t, carry):
        r, c = t // COLS, t % COLS
        picks, rows = [], []
        for k in range(4):
            own = amounts[pl.ds(pl.multiple_of((t * 4 + k) * 8, 8), 8), :]
            offset, slot = own[3:4, :], own[7:8, :]
            rows.append(jnp.concatenate([jnp.where(offset == float(o), own, 0.0) for o in range(10)], axis=0))
            picks.append(jnp.where(slot == nodes, 1.0, 0.0).astype(bf16))
        left_side = jnp.concatenate(rows, axis=1).astype(bf16)
        right_side = jnp.concatenate(picks, axis=1)
        out = lax.dot_general(left_side, right_side, (((1,), (1,)), ((), ())), preferred_element_type=f32)
        for o in range(9):
            at = pl.ds(pl.multiple_of(((r + o // 3) * EXT_COLS + c + o % 3) * 8, 8), 8)
            forces[at, :] = forces[at, :] + out[8 * o : 8 * o + 8]
        return carry

    lax.fori_loop(0, ROWS * COLS, scatter, 0, unroll=32)

    def node_sum(x, first, count, stride):
        return (
            forces[pl.ds(first * 8 + x, count, stride=8 * stride), :]
            + forces[pl.ds(first * 8 + 4 + x, count, stride=8 * stride), :]
        )

    for x in range(3):
        for r in range(ROWS):
            inner[x, r] = node_sum(x, (r + 1) * EXT_COLS + 1, COLS, 1)
        top = node_sum(x, 0, EXT_COLS, 1)
        bottom = node_sum(x, LAST * EXT_COLS, EXT_COLS, 1)
        rim_first[x] = jnp.where(even, bottom, top)
        rim_second[x] = jnp.where(even, top, bottom)
        rim_left[x] = node_sum(x, EXT_COLS, ROWS, EXT_COLS)
        rim_right[x] = node_sum(x, 2 * EXT_COLS - 1, ROWS, EXT_COLS)


def finish_body(inner, x_first, x_second, y_first, y_second, peaks, out):
    before, after = facing(x_first, x_second, "gx")
    left, right = facing(y_first, y_second, "gy")
    top = jnp.max(peaks[...])
    cols = lax.broadcasted_iota(jnp.int32, (COLS, PTS), 0)
    for x in range(3):
        west, east = left(x), right(x)
        for r in range(ROWS):
            value = inner[x, r]
            if r == 0:
                value = value + before(x)[1 : COLS + 1]
            if r == ROWS - 1:
                value = value + after(x)[1 : COLS + 1]
            value = value + jnp.where(cols == 0, west[r : r + 1], 0.0) + jnp.where(cols == COLS - 1, east[r : r + 1], 0.0)
            out[x, r] = value / top


def kernels(peers):
    f32, bf16 = jnp.float32, jnp.bfloat16
    vmem = pl.BlockSpec(memory_space=pltpu.VMEM)
    smem = pl.BlockSpec(memory_space=pltpu.SMEM)

    def call(body, name, ins, outs, scratch, flops):
        return pl.pallas_call(
            body,
            out_shape=tuple(jax.ShapeDtypeStruct(*o) for o in outs),
            in_specs=[smem if i == "links" else vmem for i in ins],
            out_specs=(vmem,) * len(outs),
            scratch_shapes=[pltpu.VMEM(*v) for v in scratch],
            compiler_params=pltpu.CompilerParams(vmem_limit_bytes=24 * MIB),
            cost_estimate=pl.CostEstimate(flops=flops, bytes_accessed=MIB, transcendentals=0),
            name=name,
        )

    split = call(
        split_body,
        "split_block",
        ("strain", "coords"),
        [
            ((TILES * PIECES, PTS), f32),
            ((EXT_COLS * PTS, PTS), bf16),
            ((EXT_COLS * ROWS * 8, PTS), f32),
            ((8, PTS), f32),
        ],
        [((TILES * PIECES, PTS), f32)],
        3 * 10**9,
    )
    inside = call(
        inside_body,
        "inside_links",
        ("links", "su", "vt", "src", "info"),
        [((8 * TILES, PTS), f32)],
        [
            ((PTS, len(INSIDE) * PTS), bf16),
            ((3 * PTS, len(INSIDE) * PTS), bf16),
        ],
        6 * 10**9,
    )
    rim = call(
        rim_body,
        "rim_links",
        ("stiff", "links", "inside", "su", "info", "x_first", "x_second", "y_first", "y_second"),
        [((LAYERS, ROWS, COLS, PTS), f32), ((ROWS, COLS, PTS), f32), ((peers, PTS), f32)],
        [
            ((EXT_COLS * PTS, PTS), f32),
            ((2 * PTS, PTS), f32),
            ((EXT_COLS * PTS, PTS), bf16),
            ((PTS, 2 * PTS), bf16),
            ((COLS * 2 * PIECES, 2 * PTS), bf16),
            ((2 * PTS, 2 * len(INSIDE) * PTS), bf16),
            ((3 * PTS * COLS + len(INSIDE) * PTS, 2 * PTS), bf16),
            ((EXT_ROWS * EXT_COLS * 8, PTS), f32),
            ((EXT_ROWS * EXT_COLS * 8, PTS), f32),
            ((8 * TILES, PTS), f32),
        ],
        4 * 10**9,
    )
    force = call(
        force_body,
        "node_forces",
        ("disp", "strength", "corners", "x_first", "x_second", "y_first", "y_second"),
        [
            ((3, ROWS, COLS, PTS), f32),
            ((3, EXT_COLS, PTS), f32),
            ((3, EXT_COLS, PTS), f32),
            ((3, ROWS, PTS), f32),
            ((3, ROWS, PTS), f32),
        ],
        [
            ((3 * EXT_ROWS * DISP_COLS, PTS), f32),
            ((TILES * 32, PTS), f32),
            ((EXT_ROWS * EXT_COLS * 8, PTS), f32),
        ],
        8 * 10**9,
    )
    finish = call(
        finish_body,
        "finish",
        ("inner", "x_first", "x_second", "y_first", "y_second", "peaks"),
        [((3, ROWS, COLS, PTS), f32)],
        [],
        10**6,
    )
    return split, inside, rim, force, finish


def swap(first, second, axis):
    peers = lax.axis_size(axis)
    with_first = [(i, i ^ 1) for i in range(peers)]
    with_second = [(i, ((i - 1) ^ 1) + 1) for i in range(1, peers - 1)]
    return lax.ppermute(first, axis, with_first), lax.ppermute(second, axis, with_second)


def local(strain, coords, displacement, stiffness, neighbours, corners):
    peers_x, peers_y = lax.axis_size("gx"), lax.axis_size("gy")
    even_x, even_y = lax.axis_index("gx") % 2 == 0, lax.axis_index("gy") % 2 == 0
    own = (coords, strain, displacement)

    def take(value, index, dim):
        return lax.dynamic_index_in_dim(value, index, dim, keepdims=False)

    def row(r):
        return jnp.concatenate([take(v, r, 1) for v in own], axis=0)

    split, inside, rim, force, finish = kernels(peers_x)
    x_halos = swap(row(jnp.where(even_x, ROWS - 1, 0)), row(jnp.where(even_x, 0, ROWS - 1)), "gx")
    pieces = split(strain, coords)
    *x_halos, pieces = lax.optimization_barrier((*x_halos, pieces))
    above = jnp.where(even_x, x_halos[1], x_halos[0])
    below = jnp.where(even_x, x_halos[0], x_halos[1])

    def column(c):
        mid = jnp.concatenate([take(v, c, 2) for v in own], axis=0)
        return jnp.concatenate([take(above, c, 1)[:, None], mid, take(below, c, 1)[:, None]], axis=1)

    y_halos = swap(column(jnp.where(even_y, COLS - 1, 0)), column(jnp.where(even_y, 0, COLS - 1)), "gy")
    own_pieces, _, _, info = pieces
    totals = inside(neighbours, *pieces)[0]
    damage, strength, peak = rim(stiffness, neighbours, totals, own_pieces, info, *x_halos, *y_halos)
    peaks = lax.all_to_all(peak, "gx", 0, 0, tiled=True)
    inner, rim_first, rim_second, rim_left, rim_right = force(displacement, strength, corners, *x_halos, *y_halos)
    rim_first, peaks = lax.optimization_barrier((rim_first, peaks))
    x_rims = swap(rim_first, rim_second, "gx")
    peaks = jnp.broadcast_to(jnp.max(peaks, axis=0, keepdims=True), (peers_y, PTS))
    peaks = lax.all_to_all(peaks, "gy", 0, 0, tiled=True)
    above = jnp.where(even_x, x_rims[1], x_rims[0])
    below = jnp.where(even_x, x_rims[0], x_rims[1])

    def side(rim_side, c):
        return rim_side.at[:, 0].add(above[:, c]).at[:, ROWS - 1].add(below[:, c])

    west, east = side(rim_left, 0), side(rim_right, EXT_COLS - 1)
    y_rims = swap(jnp.where(even_y, east, west), jnp.where(even_y, west, east), "gy")
    return damage, finish(inner, *x_rims, *y_rims, peaks)[0]


def solution(mesh):
    spec = P(None, "gx", "gy", None)
    in_specs = (spec, spec, spec, spec, P(None, "gx", "gy"), spec)
    return jax.shard_map(local, mesh=mesh, in_specs=in_specs, out_specs=(spec, spec), check_vma=False)
```

```python
import jax
import jax.numpy as jnp
from jax import lax
from jax.experimental import pallas as pl
from jax.experimental.pallas import tpu as pltpu
from jax.sharding import PartitionSpec as P

PTS = 128
LAYERS = 5
ROWS = 4
COLS = 16
EXT_ROWS = ROWS + 2
LAST = ROWS + 1
EXT_COLS = COLS + 2
STRAIN_SCALE = 0.05
INV_RADIUS = 0.1
SPREAD_LIMIT = 128.0
SLOT_OF = {(0, 0): 0, (-1, -1): 1, (-1, 0): 2, (-1, 1): 3, (0, -1): 4, (0, 1): 5, (1, -1): 6, (1, 0): 7, (1, 1): 8}
PIECES = 32
RAW = 24
TILES = ROWS * COLS
DISP_COLS = 24
INSIDE = [(o, r) for r in range(ROWS) for o in range(ROWS) if abs(o - r) <= 1]
V_ROWS = (0, 3, 6, 9, 12, 15)
MIB = 1024 * 1024


def split3(value):
    hi = value.astype(jnp.bfloat16).astype(jnp.float32)
    rest = value - hi
    mid = rest.astype(jnp.bfloat16).astype(jnp.float32)
    return hi, mid, rest - mid


def scaled(xyz, centre):
    a = [(xyz[x] - centre[x]) * INV_RADIUS for x in range(3)]
    return a, a[0] * a[0] + a[1] * a[1] + a[2] * a[2]


def centre_of(coords):
    return [0.5 * (jnp.min(coords[x]) + jnp.max(coords[x])) for x in range(3)]


def put_other(sv, a, norm, at):
    for x in range(3):
        hi, mid, lo = split3(a[x])
        for k, v in zip(V_ROWS, (hi, hi, mid, mid, hi, lo)):
            sv[at(k + x), :] = v
    for k, v in enumerate(split3(-norm)):
        sv[at(21 + k), :] = v


def put_own(su, a, norm, xyz, at):
    for x in range(3):
        hi, mid, lo = split3(a[x])
        for k, v in zip(V_ROWS, (hi, mid, hi, mid, lo, hi)):
            su[at(k + x), :] = 2.0 * v
        su[at(RAW + x), :] = xyz[x]
    for k, v in enumerate(split3(1.0 - norm)):
        su[at(18 + k), :] = v


def constant_rows():
    row8 = lax.broadcasted_iota(jnp.int32, (8, PTS), 0)
    other = jnp.where((row8 >= 2) & (row8 <= 4), 1.0, 0.0)
    own = jnp.where(row8 >= 5, 1.0, 0.0)
    ones = jnp.where(row8 == LAYERS, 1.0, 0.0)
    return other.astype(jnp.float32), own.astype(jnp.float32), ones.astype(jnp.float32)


def rows_at(index, size, count=None):
    return pl.ds(pl.multiple_of(index * size, size), size if count is None else count)


def bell_weights(other, own):
    bell = jnp.maximum(jnp.dot(other, own, preferred_element_type=jnp.float32), 0.0)
    return (bell * bell).astype(jnp.bfloat16)


def direct_total(own, other, values):
    turned = jnp.concatenate([other] + [jnp.zeros((8, PTS), jnp.float32)] * 15, axis=0).T
    dist = jnp.zeros((PTS, PTS), jnp.float32)
    for x in range(3):
        dist = dist + (own[x : x + 1, :] - turned[:, x : x + 1]) ** 2
    bell = jnp.maximum(1.0 - dist * 0.01, 0.0)
    pair = (bell * bell).astype(jnp.bfloat16)
    return jnp.dot(values.astype(jnp.bfloat16), pair, preferred_element_type=jnp.float32)


def is_live(links, dr, dc, r, c):
    return jnp.where(links[SLOT_OF[(dr, dc)], r, c] >= 0, 1.0, 0.0).astype(jnp.float32)


def facing(first, second, axis):
    even = lax.axis_index(axis) % 2 == 0
    return (lambda i: jnp.where(even, second[i], first[i])), (lambda i: jnp.where(even, first[i], second[i]))


def split_body(strain, coords, su, vt, src, info, sv):
    f32, bf16 = jnp.float32, jnp.bfloat16
    other_const, own_const, ones = constant_rows()
    zero8 = jnp.zeros((8, PTS), f32)
    for c in range(EXT_COLS):
        edge = c in (0, EXT_COLS - 1)
        for r in range(ROWS):
            src[pl.ds((c * ROWS + r) * 8, 8), :] = zero8 if edge else ones
            if not edge:
                sv[pl.ds(((c - 1) * ROWS + r) * PIECES + 16, 8), :] = other_const
                sv[pl.ds(((c - 1) * ROWS + r) * PIECES + 24, 8), :] = zero8
    for t in range(TILES):
        su[pl.ds(t * PIECES + 16, 8), :] = own_const
        su[pl.ds(t * PIECES + 24, 8), :] = zero8
    for c in (0, EXT_COLS - 1):
        vt[pl.ds(c * PTS, PTS), :] = jnp.zeros((PTS, PTS), bf16)

    centre = centre_of(coords)
    far = jnp.zeros((COLS, PTS), f32)
    step = ROWS * PIECES
    for r in range(ROWS):
        xyz = [coords[x, r] for x in range(3)]
        a, norm = scaled(xyz, centre)
        far = jnp.maximum(far, norm)
        put_other(sv, a, norm, lambda k: pl.ds(r * PIECES + k, COLS, stride=step))
        put_own(su, a, norm, xyz, lambda k: pl.ds(r * PIECES + k, COLS, stride=step))
        for l in range(LAYERS):
            src[pl.ds((ROWS + r) * 8 + l, COLS, stride=ROWS * 8), :] = strain[l, r]
    info[...] = jnp.zeros(info.shape, f32)
    for x in range(3):
        info[x : x + 1] = jnp.full((1, PTS), centre[x], f32)
    info[3:4] = jnp.max(far, axis=0, keepdims=True)

    def turn(c, carry):
        vt[rows_at(c + 1, PTS), :] = sv[rows_at(c, step), :].T.astype(bf16)
        return carry

    lax.fori_loop(0, COLS, turn, 0, unroll=16)


def inside_body(links, su, vt, src, info, totals, block, weights):
    f32, bf16 = jnp.float32, jnp.bfloat16
    zero8 = jnp.zeros((8, PTS), f32)
    block[...] = jnp.zeros(block.shape, bf16)
    near = jnp.max(info[3:4]) <= SPREAD_LIMIT

    @pl.when(near)
    def _():
        def column(c, carry):
            for j, (o, r) in enumerate(INSIDE):
                own = su[rows_at(c * ROWS + r, PIECES), :]
                block[pl.ds(o * PIECES, PIECES), pl.ds(j * PTS, PTS)] = own.astype(bf16)
            others = vt[rows_at(c, PTS, 3 * PTS), :]
            for j in range(0, len(INSIDE), 2):
                weights[:, j * PTS : (j + 2) * PTS] = bell_weights(others, block[:, j * PTS : (j + 2) * PTS])
            sums = [zero8 for _ in range(ROWS)]
            for j in range(0, len(INSIDE), 2):
                halves = []
                for o, r in INSIDE[j : j + 2]:
                    parts = [src[rows_at((c + dc) * ROWS + o, 8), :] * is_live(links, o - r, dc - 1, r, c) for dc in range(3)]
                    halves.append(jnp.concatenate(parts, axis=1))
                values = jnp.concatenate(halves, axis=0).astype(bf16)
                out = jnp.dot(values, weights[:, j * PTS : (j + 2) * PTS], preferred_element_type=f32)
                for h in range(2):
                    r = INSIDE[j + h][1]
                    sums[r] = sums[r] + out[8 * h : 8 * h + 8, h * PTS : (h + 1) * PTS]
            for r in range(ROWS):
                totals[pl.ds(r * COLS + c, 8, stride=TILES), :] = sums[r]
            return carry

        lax.fori_loop(0, COLS, column, 0, unroll=16)

    @pl.when(jnp.logical_not(near))
    def _():
        def tile(t, carry):
            r, c = t // COLS, t % COLS
            own = su[pl.ds(pl.multiple_of((c * ROWS + r) * PIECES + RAW, 8), 8), :]
            total = zero8
            for (dr, dc), slot in SLOT_OF.items():
                within = (r + dr >= 0) & (r + dr < ROWS) & (c + dc >= 0) & (c + dc < COLS) & (links[slot, r, c] >= 0)
                o = jnp.minimum(jnp.maximum(r + dr, 0), ROWS - 1)
                oc = jnp.minimum(jnp.maximum(c + dc, 0), COLS - 1)
                other = su[pl.ds(pl.multiple_of((oc * ROWS + o) * PIECES + RAW, 8), 8), :]
                values = src[rows_at((oc + 1) * ROWS + o, 8), :] * jnp.where(within, 1.0, 0.0)
                total = total + direct_total(own, other, values)
            totals[pl.ds(t, 8, stride=TILES), :] = total
            return carry

        lax.fori_loop(0, TILES, tile, 0)


def rim_body(
    stiff, links, inside, su, info, x_first, x_second, y_first, y_second,
    damage, strength, peak,
    sv, sides, vt, vt_sides, block, block_sides, weights, src, raw, totals,
):
    before, after = facing(x_first, x_second, "gx")
    left, right = facing(y_first, y_second, "gy")
    f32, bf16 = jnp.float32, jnp.bfloat16
    gx, gy = lax.axis_index("gx"), lax.axis_index("gy")
    has_top, has_bot = gx > 0, gx < lax.axis_size("gx") - 1
    has_left, has_right = gy > 0, gy < lax.axis_size("gy") - 1
    other_const, _, ones = constant_rows()
    zero8 = jnp.zeros((8, PTS), f32)
    totals[...] = inside[...]
    for c in range(EXT_COLS):
        for h in range(2):
            sv[pl.ds((2 * c + h) * PIECES + 16, 8), :] = other_const
            sv[pl.ds((2 * c + h) * PIECES + 24, 8), :] = zero8
            src[pl.ds(((h * LAST) * EXT_COLS + c) * 8, 8), :] = ones
    for r in range(ROWS):
        for h in range(2):
            sides[pl.ds((h * ROWS + r) * PIECES + 16, 8), :] = other_const
            sides[pl.ds((h * ROWS + r) * PIECES + 24, 8), :] = zero8
            src[pl.ds(((r + 1) * EXT_COLS + h * (EXT_COLS - 1)) * 8, 8), :] = ones
    block[...] = jnp.zeros(block.shape, bf16)
    block_sides[...] = jnp.zeros(block_sides.shape, bf16)

    centre = [info[x : x + 1, :] for x in range(3)]
    far = jnp.broadcast_to(info[3:4, :], (COLS, PTS))
    for h, halo, there in ((0, before, has_top), (1, after, has_bot)):
        xyz = [halo(x) for x in range(3)]
        a, norm = scaled(xyz, centre)
        far = jnp.maximum(far, jnp.where(there, norm, 0.0))
        put_other(sv, a, norm, lambda k: pl.ds((2 + h) * PIECES + k, COLS, stride=2 * PIECES))
        first = (h * LAST * EXT_COLS + 1) * 8
        for x in range(3):
            raw[pl.ds(first + x, COLS, stride=8), :] = xyz[x]
        for l in range(LAYERS):
            src[pl.ds(first + l, COLS, stride=8), :] = halo(3 + l)
    rows6 = lax.broadcasted_iota(jnp.int32, (EXT_ROWS, PTS), 0)
    there6 = ((rows6 > 0) | has_top) & ((rows6 < LAST) | has_bot)
    side = jnp.zeros((EXT_ROWS, PTS), f32)
    for h, halo, there in ((0, left, has_left), (1, right, has_right)):
        xyz = [halo(x) for x in range(3)]
        a, norm = scaled(xyz, centre)
        side = jnp.maximum(side, jnp.where(there6 & there, norm, 0.0))
        mid = [v[1:LAST] for v in a]
        put_other(sides, mid, norm[1:LAST], lambda k: pl.ds(h * ROWS * PIECES + k, ROWS, stride=PIECES))
        col = h * (EXT_COLS - 1)
        for e in range(2):
            one = slice(e * LAST, e * LAST + 1)
            put_other(sv, [v[one] for v in a], norm[one], lambda k: pl.ds((2 * col + e) * PIECES + k, 1))
        for x in range(3):
            raw[pl.ds(col * 8 + x, EXT_ROWS, stride=EXT_COLS * 8), :] = xyz[x]
        for l in range(LAYERS):
            src[pl.ds(col * 8 + l, EXT_ROWS, stride=EXT_COLS * 8), :] = halo(3 + l)
    near = jnp.maximum(jnp.max(far), jnp.max(side)) <= SPREAD_LIMIT

    def add(r, c, value):
        at = pl.ds(r * COLS + c, 8, stride=TILES)
        totals[at, :] = totals[at, :] + value

    @pl.when(near)
    def _():
        def turn(c, carry):
            vt[rows_at(c, PTS), :] = sv[rows_at(c, 2 * PIECES), :].T.astype(bf16)
            return carry

        lax.fori_loop(0, EXT_COLS, turn, 0, unroll=18)
        vt_sides[...] = sides[...].T.astype(bf16)
        for h in range(2):
            for j, (o, r) in enumerate(INSIDE):
                own = su[pl.ds((h * (COLS - 1) * ROWS + r) * PIECES, PIECES), :].astype(bf16)
                block_sides[pl.ds((h * ROWS + o) * PIECES, PIECES), pl.ds((h * len(INSIDE) + j) * PTS, PTS)] = own
        for j in range(0, 2 * len(INSIDE), 2):
            weights[pl.ds(3 * PTS * COLS + (j // 2) * PTS, PTS), :] = bell_weights(
                vt_sides[...], block_sides[:, j * PTS : (j + 2) * PTS]
            )

        def weigh(c, carry):
            for h in range(2):
                own = su[rows_at(c * ROWS + h * (ROWS - 1), PIECES), :].astype(bf16)
                block[rows_at(2 * c + h, PIECES), pl.ds(h * PTS, PTS)] = own
            own = block[rows_at(c, 2 * PIECES), :]
            weights[rows_at(c, 3 * PTS), :] = bell_weights(vt[rows_at(c, PTS, 3 * PTS), :], own)
            return carry

        lax.fori_loop(0, COLS, weigh, 0, unroll=16)

        def total(c, carry):
            halves = []
            for h in range(2):
                parts = [
                    src[rows_at(h * LAST * EXT_COLS + c + dc, 8), :] * is_live(links, 2 * h - 1, dc - 1, h * (ROWS - 1), c)
                    for dc in range(3)
                ]
                halves.append(jnp.concatenate(parts, axis=1))
            values = jnp.concatenate(halves, axis=0).astype(bf16)
            out = jnp.dot(values, weights[rows_at(c, 3 * PTS), :], preferred_element_type=f32)
            for h in range(2):
                add(h * (ROWS - 1), c, out[8 * h : 8 * h + 8, h * PTS : (h + 1) * PTS])
            return carry

        lax.fori_loop(0, COLS, total, 0, unroll=16)
        sums = [[zero8 for _ in range(ROWS)] for _ in range(2)]
        for j in range(0, 2 * len(INSIDE), 2):
            halves, owners = [], []
            for i in (j, j + 1):
                h, (o, r) = i // len(INSIDE), INSIDE[i % len(INSIDE)]
                held = src[pl.ds(((o + 1) * EXT_COLS + h * (EXT_COLS - 1)) * 8, 8), :]
                halves.append(held * is_live(links, o - r, 2 * h - 1, r, h * (COLS - 1)))
                owners.append((h, r))
            values = jnp.concatenate(halves, axis=0).astype(bf16)
            pair = weights[pl.ds(3 * PTS * COLS + (j // 2) * PTS, PTS), :]
            out = jnp.dot(values, pair, preferred_element_type=f32)
            for i, (h, r) in enumerate(owners):
                sums[h][r] = sums[h][r] + out[8 * i : 8 * i + 8, i * PTS : (i + 1) * PTS]
        for h in range(2):
            for r in range(ROWS):
                add(r, h * (COLS - 1), sums[h][r])

    @pl.when(jnp.logical_not(near))
    def _():
        def tile(t, carry):
            r, c = t // COLS, t % COLS
            own = su[pl.ds(pl.multiple_of((c * ROWS + r) * PIECES + RAW, 8), 8), :]
            for (dr, dc), slot in SLOT_OF.items():
                o, oc = r + dr, c + dc
                within = (o >= 0) & (o < ROWS) & (oc >= 0) & (oc < COLS)

                @pl.when(jnp.logical_not(within) & (links[slot, r, c] >= 0))
                def _():
                    at = rows_at((o + 1) * EXT_COLS + oc + 1, 8)
                    add(r, c, direct_total(own, raw[at, :], src[at, :]))

            return carry

        lax.fori_loop(0, TILES, tile, 0)

    for r in range(ROWS):
        weight_sum = totals[pl.ds(LAYERS * TILES + r * COLS, COLS), :]
        mean = jnp.zeros((COLS, PTS), f32)
        for l in range(LAYERS):
            averaged = totals[pl.ds(l * TILES + r * COLS, COLS), :] / weight_sum
            value = averaged / (averaged + STRAIN_SCALE)
            damage[l, r] = value
            mean = mean + value
        power = (1.0 - mean / LAYERS) * stiff[0, r]
        strength[r] = power
        top = jnp.maximum(top, power) if r else power
    peak[...] = jnp.full(peak.shape, jnp.max(top), f32)


def force_body(
    disp, strength, corners, x_first, x_second, y_first, y_second,
    inner, rim_first, rim_second, rim_left, rim_right,
    edisp, amounts, forces,
):
    f32, bf16 = jnp.float32, jnp.bfloat16
    before, after = facing(x_first, x_second, "gx")
    left, right = facing(y_first, y_second, "gy")
    even = lax.axis_index("gx") % 2 == 0
    forces[...] = jnp.zeros(forces.shape, f32)
    for x in range(3):
        for r in range(EXT_ROWS):
            row = before(8 + x) if r == 0 else after(8 + x) if r == LAST else disp[x, r - 1]
            edisp[pl.ds((x * EXT_ROWS + r) * DISP_COLS + 1, COLS), :] = row
        edisp[pl.ds(x * EXT_ROWS * DISP_COLS, EXT_ROWS, stride=DISP_COLS), :] = left(8 + x)
        edisp[pl.ds(x * EXT_ROWS * DISP_COLS + COLS + 1, EXT_ROWS, stride=DISP_COLS), :] = right(8 + x)

    def gather(r, carry):
        for g in range(COLS // 8):
            power = strength[r, 8 * g : 8 * g + 8, :]
            codes = [corners[k, r, 8 * g : 8 * g + 8, :] for k in range(4)]
            offset = [code >> 7 for code in codes]
            slot = [code & (PTS - 1) for code in codes]
            at = [
                pl.ds(pl.multiple_of(((r * COLS + 8 * g) * 4 + k) * 8, 8) + i, 8, stride=32)
                for k in range(4) for i in range(8)
            ]
            for k in range(4):
                amounts[at[8 * k + 3], :] = offset[k].astype(f32)
                amounts[at[8 * k + 7], :] = slot[k].astype(f32)
            for x in range(3):
                picked = []
                base = (x * EXT_ROWS + r) * DISP_COLS + 8 * g
                table = [edisp[pl.ds(base + (o // 3) * DISP_COLS + o % 3, 8), :] for o in range(9)]
                for k in range(4):
                    found = jnp.take_along_axis(table[0], slot[k], axis=1)
                    for o in range(1, 9):
                        found = jnp.where(offset[k] == o, jnp.take_along_axis(table[o], slot[k], axis=1), found)
                    picked.append(found)
                springs = [power * (picked[(k + 1) % 4] - picked[k]) for k in range(4)]
                for k in range(4):
                    amount = springs[k] - springs[(k + 3) % 4]
                    hi = amount.astype(bf16).astype(f32)
                    amounts[at[8 * k + x], :] = hi
                    amounts[at[8 * k + 4 + x], :] = amount - hi
        return carry

    lax.fori_loop(0, ROWS, gather, 0, unroll=4)

    nodes = lax.broadcasted_iota(jnp.int32, (PTS, PTS), 0).astype(f32)

    def scatter(t, carry):
        r, c = t // COLS, t % COLS
        picks, rows = [], []
        for k in range(4):
            own = amounts[pl.ds(pl.multiple_of((t * 4 + k) * 8, 8), 8), :]
            offset, slot = own[3:4, :], own[7:8, :]
            rows.append(jnp.concatenate([jnp.where(offset == float(o), own, 0.0) for o in range(10)], axis=0))
            picks.append(jnp.where(slot == nodes, 1.0, 0.0).astype(bf16))
        left_side = jnp.concatenate(rows, axis=1).astype(bf16)
        right_side = jnp.concatenate(picks, axis=1)
        out = lax.dot_general(left_side, right_side, (((1,), (1,)), ((), ())), preferred_element_type=f32)
        for o in range(9):
            at = pl.ds(pl.multiple_of(((r + o // 3) * EXT_COLS + c + o % 3) * 8, 8), 8)
            forces[at, :] = forces[at, :] + out[8 * o : 8 * o + 8]
        return carry

    lax.fori_loop(0, ROWS * COLS, scatter, 0, unroll=32)

    def node_sum(x, first, count, stride):
        return (
            forces[pl.ds(first * 8 + x, count, stride=8 * stride), :]
            + forces[pl.ds(first * 8 + 4 + x, count, stride=8 * stride), :]
        )

    for x in range(3):
        for r in range(ROWS):
            inner[x, r] = node_sum(x, (r + 1) * EXT_COLS + 1, COLS, 1)
        top = node_sum(x, 0, EXT_COLS, 1)
        bottom = node_sum(x, LAST * EXT_COLS, EXT_COLS, 1)
        rim_first[x] = jnp.where(even, bottom, top)
        rim_second[x] = jnp.where(even, top, bottom)
        rim_left[x] = node_sum(x, EXT_COLS, ROWS, EXT_COLS)
        rim_right[x] = node_sum(x, 2 * EXT_COLS - 1, ROWS, EXT_COLS)


def finish_body(inner, x_first, x_second, y_first, y_second, peaks, out):
    before, after = facing(x_first, x_second, "gx")
    left, right = facing(y_first, y_second, "gy")
    top = jnp.max(peaks[...])
    cols = lax.broadcasted_iota(jnp.int32, (COLS, PTS), 0)
    for x in range(3):
        west, east = left(x), right(x)
        for r in range(ROWS):
            value = inner[x, r]
            if r == 0:
                value = value + before(x)[1 : COLS + 1]
            if r == ROWS - 1:
                value = value + after(x)[1 : COLS + 1]
            value = value + jnp.where(cols == 0, west[r : r + 1], 0.0) + jnp.where(cols == COLS - 1, east[r : r + 1], 0.0)
            out[x, r] = value / top


def kernels(peers):
    f32, bf16 = jnp.float32, jnp.bfloat16
    vmem = pl.BlockSpec(memory_space=pltpu.VMEM)
    smem = pl.BlockSpec(memory_space=pltpu.SMEM)

    def call(body, name, ins, outs, scratch, flops):
        return pl.pallas_call(
            body,
            out_shape=tuple(jax.ShapeDtypeStruct(*o) for o in outs),
            in_specs=[smem if i == "links" else vmem for i in ins],
            out_specs=(vmem,) * len(outs),
            scratch_shapes=[pltpu.VMEM(*v) for v in scratch],
            compiler_params=pltpu.CompilerParams(vmem_limit_bytes=24 * MIB),
            cost_estimate=pl.CostEstimate(flops=flops, bytes_accessed=MIB, transcendentals=0),
            name=name,
        )

    split = call(
        split_body,
        "split_block",
        ("strain", "coords"),
        [
            ((TILES * PIECES, PTS), f32),
            ((EXT_COLS * PTS, PTS), bf16),
            ((EXT_COLS * ROWS * 8, PTS), f32),
            ((8, PTS), f32),
        ],
        [((TILES * PIECES, PTS), f32)],
        3 * 10**9,
    )
    inside = call(
        inside_body,
        "inside_links",
        ("links", "su", "vt", "src", "info"),
        [((8 * TILES, PTS), f32)],
        [
            ((PTS, len(INSIDE) * PTS), bf16),
            ((3 * PTS, len(INSIDE) * PTS), bf16),
        ],
        6 * 10**9,
    )
    rim = call(
        rim_body,
        "rim_links",
        ("stiff", "links", "inside", "su", "info", "x_first", "x_second", "y_first", "y_second"),
        [((LAYERS, ROWS, COLS, PTS), f32), ((ROWS, COLS, PTS), f32), ((peers, PTS), f32)],
        [
            ((EXT_COLS * 2 * PIECES, PTS), f32),
            ((2 * PTS, PTS), f32),
            ((EXT_COLS * PTS, 2 * PIECES), bf16),
            ((PTS, 2 * PTS), bf16),
            ((COLS * 2 * PIECES, 2 * PTS), bf16),
            ((2 * PTS, 2 * len(INSIDE) * PTS), bf16),
            ((3 * PTS * COLS + len(INSIDE) * PTS, 2 * PTS), bf16),
            ((EXT_ROWS * EXT_COLS * 8, PTS), f32),
            ((EXT_ROWS * EXT_COLS * 8, PTS), f32),
            ((8 * TILES, PTS), f32),
        ],
        4 * 10**9,
    )
    force = call(
        force_body,
        "node_forces",
        ("disp", "strength", "corners", "x_first", "x_second", "y_first", "y_second"),
        [
            ((3, ROWS, COLS, PTS), f32),
            ((3, EXT_COLS, PTS), f32),
            ((3, EXT_COLS, PTS), f32),
            ((3, ROWS, PTS), f32),
            ((3, ROWS, PTS), f32),
        ],
        [
            ((3 * EXT_ROWS * DISP_COLS, PTS), f32),
            ((TILES * 32, PTS), f32),
            ((EXT_ROWS * EXT_COLS * 8, PTS), f32),
        ],
        8 * 10**9,
    )
    finish = call(
        finish_body,
        "finish",
        ("inner", "x_first", "x_second", "y_first", "y_second", "peaks"),
        [((3, ROWS, COLS, PTS), f32)],
        [],
        10**6,
    )
    return split, inside, rim, force, finish


def swap(first, second, axis):
    peers = lax.axis_size(axis)
    with_first = [(i, i ^ 1) for i in range(peers)]
    with_second = [(i, ((i - 1) ^ 1) + 1) for i in range(1, peers - 1)]
    return lax.ppermute(first, axis, with_first), lax.ppermute(second, axis, with_second)


def local(strain, coords, displacement, stiffness, neighbours, corners):
    peers_x, peers_y = lax.axis_size("gx"), lax.axis_size("gy")
    even_x, even_y = lax.axis_index("gx") % 2 == 0, lax.axis_index("gy") % 2 == 0
    own = (coords, strain, displacement)

    def take(value, index, dim):
        return lax.dynamic_index_in_dim(value, index, dim, keepdims=False)

    def row(r):
        return jnp.concatenate([take(v, r, 1) for v in own], axis=0)

    split, inside, rim, force, finish = kernels(peers_x)
    x_halos = swap(row(jnp.where(even_x, ROWS - 1, 0)), row(jnp.where(even_x, 0, ROWS - 1)), "gx")
    pieces = split(strain, coords)
    *x_halos, pieces = lax.optimization_barrier((*x_halos, pieces))
    above = jnp.where(even_x, x_halos[1], x_halos[0])
    below = jnp.where(even_x, x_halos[0], x_halos[1])

    def column(c):
        mid = jnp.concatenate([take(v, c, 2) for v in own], axis=0)
        return jnp.concatenate([take(above, c, 1)[:, None], mid, take(below, c, 1)[:, None]], axis=1)

    y_halos = swap(column(jnp.where(even_y, COLS - 1, 0)), column(jnp.where(even_y, 0, COLS - 1)), "gy")
    own_pieces, _, _, info = pieces
    totals = inside(neighbours, *pieces)[0]
    damage, strength, peak = rim(stiffness, neighbours, totals, own_pieces, info, *x_halos, *y_halos)
    peaks = lax.all_to_all(peak, "gx", 0, 0, tiled=True)
    inner, rim_first, rim_second, rim_left, rim_right = force(displacement, strength, corners, *x_halos, *y_halos)
    rim_first, peaks = lax.optimization_barrier((rim_first, peaks))
    x_rims = swap(rim_first, rim_second, "gx")
    peaks = jnp.broadcast_to(jnp.max(peaks, axis=0, keepdims=True), (peers_y, PTS))
    peaks = lax.all_to_all(peaks, "gy", 0, 0, tiled=True)
    above = jnp.where(even_x, x_rims[1], x_rims[0])
    below = jnp.where(even_x, x_rims[0], x_rims[1])

    def side(rim_side, c):
        return rim_side.at[:, 0].add(above[:, c]).at[:, ROWS - 1].add(below[:, c])

    west, east = side(rim_left, 0), side(rim_right, EXT_COLS - 1)
    y_rims = swap(jnp.where(even_y, east, west), jnp.where(even_y, west, east), "gy")
    return damage, finish(inner, *x_rims, *y_rims, peaks)[0]


def solution(mesh):
    spec = P(None, "gx", "gy", None)
    in_specs = (spec, spec, spec, spec, P(None, "gx", "gy"), spec)
    return jax.shard_map(local, mesh=mesh, in_specs=in_specs, out_specs=(spec, spec), check_vma=False)
```
